128 devices in a mesh: row: 8 (over y, core), col: 16 (over z, x).
Axes of the slice: x: 4, y: 4, z: 4, core: 2. Of those that a mesh axis runs over, the one named last changes fastest.
Arguments:
- patches: float32 [64, 128, 2, 128, 128], P('row', 'col'), may hold values from -6 to 6
- right_offset: int32 [64, 128], P('row', 'col'), may hold values from 57 to 112, as said below
- right_width: int32 [64, 128], P('row', 'col'), may hold values from 16 to 64
- down_offset: int32 [64, 128], P('row', 'col'), may hold values from 57 to 112, as said below
- down_width: int32 [64, 128], P('row', 'col'), may hold values from 16 to 64
Outputs:
- blended: float32 [64, 128, 2, 128, 128], P('row', 'col')
- phases: float32 [2, 64, 128], P(None, 'row', 'col')
The draws below stay inside these ranges and needn't reach their ends.
Inputs may be any that keep to these rules, and one draw needn't show every extreme that they name: right_offset + right_width lies above 120 and at most 128. down_offset + down_width lies above 120 and at most 128.
All inputs are finite; a program needn't handle non-finite values.
Results may differ from the reference program's by a relative error of at most 0.0003.
Values sent between devices are 32-bit elements; how exact they have to be, the bound alone decides.
No kernel may reach another device: no remote copies, remote signals or barrier semaphores. Data moves between devices by JAX's collectives and lax.ppermute only.
A program may use at most 128 MiB of HBM per device.

```python
import jax
import jax.numpy as jnp
from jax import lax

PATCH = 128
STRIP_MIN = 16
STRIP_MAX = 64
JITTER = 8
ITERS = 2
GRID_ROWS = 64
GRID_COLS = 128


def draw_patches(key, part):
    shape = (GRID_ROWS, GRID_COLS, 2, PATCH, PATCH)
    return jnp.clip(jax.random.normal(jax.random.fold_in(key, 5), shape, jnp.float32), -6.0, 6.0)


def strip_table(key, salt):
    base = jax.random.fold_in(key, salt)
    width_key, jitter_key = jax.random.split(base)
    width = jax.random.randint(width_key, (GRID_ROWS, GRID_COLS), STRIP_MIN, STRIP_MAX + 1)
    jitter = jax.random.randint(jitter_key, (GRID_ROWS, GRID_COLS), 0, JITTER)
    width = width.at[0, 0].set(STRIP_MAX).at[1, 1].set(STRIP_MIN)
    jitter = jitter.at[0, 0].set(JITTER - 1).at[1, 1].set(0)
    return (width.astype(jnp.int32), (PATCH - width - jitter).astype(jnp.int32))


def draw_right_offset(key, part):
    return strip_table(key, 11)[1]


def draw_right_width(key, part):
    return strip_table(key, 11)[0]


def draw_down_offset(key, part):
    return strip_table(key, 23)[1]


def draw_down_width(key, part):
    return strip_table(key, 23)[0]


def setup_inputs(seed: int = 0) -> dict:
    seeds = jax.random.split(jax.random.key(seed), 6)
    return {
        "patches": draw_patches(jax.random.fold_in(seeds[5], 71), 0),
        "right_offset": draw_right_offset(jax.random.fold_in(seeds[5], 71), 0),
        "right_width": draw_right_width(jax.random.fold_in(seeds[5], 71), 0),
        "down_offset": draw_down_offset(jax.random.fold_in(seeds[5], 71), 0),
        "down_width": draw_down_width(jax.random.fold_in(seeds[5], 71), 0),
    }


eps_norm = 1.0

def gather_lanes(field, index, axis):
    return jnp.take_along_axis(field, jnp.broadcast_to(index, field.shape), axis=axis)

def correlate(shifted, partner, width_table):
    real_part = lax.optimization_barrier(jnp.sum(shifted[..., 0, :, :] * partner[..., 0, :, :] + shifted[..., 1, :, :] * partner[..., 1, :, :], axis=(-2, -1)))
    imag_part = lax.optimization_barrier(jnp.sum(shifted[..., 0, :, :] * partner[..., 1, :, :] - shifted[..., 1, :, :] * partner[..., 0, :, :], axis=(-2, -1)))
    scale = 1.0 / jnp.sqrt(PATCH * width_table.astype(jnp.float32))
    return jnp.stack([real_part * scale, imag_part * scale])

def complex_times(factor, field):
    return jnp.stack([factor[0] * field[0] - factor[1] * field[1], factor[0] * field[1] + factor[1] * field[0]])

def conj_times(factor, field):
    return jnp.stack([factor[0] * field[0] + factor[1] * field[1], factor[0] * field[1] - factor[1] * field[0]])

def rotate(factor, field):
    real_part = factor[..., 0:1, :, :] * field[..., 0:1, :, :] - factor[..., 1:2, :, :] * field[..., 1:2, :, :]
    imag_part = factor[..., 0:1, :, :] * field[..., 1:2, :, :] + factor[..., 1:2, :, :] * field[..., 0:1, :, :]
    return jnp.concatenate([real_part, imag_part], axis=-3)

def from_east(field):
    return jnp.pad(field[:, :, 1:], ((0, 0), (0, 0), (0, 1)))

def from_south(field):
    return jnp.pad(field[:, 1:, :], ((0, 0), (0, 1), (0, 0)))

def from_west(field):
    return jnp.pad(field[:, :, :-1], ((0, 0), (0, 0), (1, 0)))

def from_north(field):
    return jnp.pad(field[:, :-1, :], ((0, 0), (1, 0), (0, 0)))

def reference(patches, right_offset, right_width, down_offset, down_width):
    lane_index = jnp.arange(PATCH, dtype=jnp.int32)

    def row_fields(row):
        here = lax.dynamic_index_in_dim(patches, row, 0, False)
        below = lax.dynamic_index_in_dim(patches, jnp.minimum(row + 1, GRID_ROWS - 1).astype(jnp.int32), 0, False)
        below = below * jnp.where(row + 1 < GRID_ROWS, 1.0, 0.0).astype(jnp.float32)
        east = jnp.concatenate([here[1:], jnp.zeros_like(here[:1])], axis=0)
        east_off = lax.dynamic_index_in_dim(right_offset, row, 0, False)
        east_wid = lax.dynamic_index_in_dim(right_width, row, 0, False)
        south_off = lax.dynamic_index_in_dim(down_offset, row, 0, False)
        south_wid = lax.dynamic_index_in_dim(down_width, row, 0, False)
        return (here, below, east, east_off, east_wid, south_off, south_wid)

    def corr_row(row):
        here, below, east, east_off, east_wid, south_off, south_wid = row_fields(row)
        east_index = jnp.clip(lane_index[None, :] + east_off[:, None], 0, PATCH - 1)
        east_keep = (lane_index[None, :] < east_wid[:, None]).astype(jnp.float32)
        east_shifted = gather_lanes(here, east_index[:, None, None, :], 3) * east_keep[:, None, None, :]
        south_index = jnp.clip(lane_index[None, :] + south_off[:, None], 0, PATCH - 1)
        south_keep = (lane_index[None, :] < south_wid[:, None]).astype(jnp.float32)
        south_shifted = gather_lanes(here, south_index[:, None, :, None], 2) * south_keep[:, None, :, None]
        return jnp.concatenate([correlate(east_shifted, east, east_wid), correlate(south_shifted, below, south_wid)])
    rows = jnp.arange(GRID_ROWS, dtype=jnp.int32)
    corr = jnp.transpose(lax.map(corr_row, rows), (1, 0, 2))
    corr_east = corr[0:2]
    corr_south = corr[2:4]
    phase_now = jnp.stack([jnp.ones((GRID_ROWS, GRID_COLS), jnp.float32), jnp.zeros((GRID_ROWS, GRID_COLS), jnp.float32)])
    for step in range(ITERS):
        image = complex_times(corr_east, from_east(phase_now)) + complex_times(corr_south, from_south(phase_now))
        image = image + conj_times(from_west(corr_east), from_west(phase_now)) + conj_times(from_north(corr_south), from_north(phase_now))
        mean_square = jnp.sum(image * image) / (GRID_ROWS * GRID_COLS)
        phase_now = image / jnp.sqrt(mean_square + eps_norm)
    east_phase = from_east(phase_now)
    south_phase = from_south(phase_now)
    col_live = (jnp.arange(GRID_COLS, dtype=jnp.int32) < GRID_COLS - 1).astype(jnp.float32)

    def blend_row(row):
        here, below, east, east_off, east_wid, south_off, south_wid = row_fields(row)
        east_index = jnp.clip(lane_index[None, :] - east_off[:, None], 0, PATCH - 1)
        east_mask = ((lane_index[None, :] >= east_off[:, None]) & (lane_index[None, :] < east_off[:, None] + east_wid[:, None])).astype(jnp.float32)
        east_place = gather_lanes(east, east_index[:, None, None, :], 3) * east_mask[:, None, None, :]
        south_index = jnp.clip(lane_index[None, :] - south_off[:, None], 0, PATCH - 1)
        south_mask = ((lane_index[None, :] >= south_off[:, None]) & (lane_index[None, :] < south_off[:, None] + south_wid[:, None])).astype(jnp.float32)
        south_place = gather_lanes(below, south_index[:, None, :, None], 2) * south_mask[:, None, :, None]
        own = jnp.transpose(lax.dynamic_index_in_dim(phase_now, row, 1, False))[:, :, None, None]
        east_factor = jnp.transpose(lax.dynamic_index_in_dim(east_phase, row, 1, False))[:, :, None, None]
        south_factor = jnp.transpose(lax.dynamic_index_in_dim(south_phase, row, 1, False))[:, :, None, None]
        numer = rotate(own, here) + rotate(east_factor, east_place) + rotate(south_factor, south_place)
        south_live = jnp.where(row + 1 < GRID_ROWS, 1.0, 0.0).astype(jnp.float32)
        weight = 1.0 + (east_mask * col_live[:, None])[:, None, None, :] + (south_mask * south_live)[:, None, :, None]
        return numer / weight
    blended = lax.map(blend_row, rows)
    return (blended, phase_now)
```

```python
import functools

import jax
import jax.numpy as jnp
from jax import lax
from jax.experimental import pallas as pl
from jax.experimental.pallas import tpu as pltpu
from jax.sharding import PartitionSpec as P

ITERS = 2
EPS_NORM = 1.0
SIDE = 128
HALF = 64
ROW0 = 56
PAD = 8
HIGHEST = lax.Precision.HIGHEST


def lanes(shape):
    return lax.broadcasted_iota(jnp.int32, shape, len(shape) - 1)


def fold8(x):
    total = x[0:8]
    for k in range(8, x.shape[0], 8):
        total = total + x[k : k + 8]
    return total


def products(ar, ai, br, bi):
    return fold8(ar * br + ai * bi), fold8(ar * bi - ai * br)


def placed_rows(pad_ref, j, part, first, offset):
    start = jnp.maximum(first - offset, -PAD) + PAD
    return pad_ref[j, part, pl.ds(start, 8), :]


def east_sums(a_real, a_imag, b_real, b_imag, offset, width):
    real, imag = None, None
    for k in range(0, SIDE, 32):
        pr, pi = products(a_real(k), a_imag(k), b_real(k), b_imag(k))
        real = pr if real is None else real + pr
        imag = pi if imag is None else imag + pi
    lane = lanes((8, SIDE))
    keep = (lane >= offset) & (lane < offset + width)
    return jnp.where(keep, real, 0.0), jnp.where(keep, imag, 0.0)


def south_sums(a_ref_at, pad_ref, j, offset, width):
    row = lax.broadcasted_iota(jnp.int32, (8, SIDE), 0)
    real = jnp.zeros((8, SIDE), jnp.float32)
    imag = real
    for first in range(ROW0, SIDE, 8):
        at = row + first
        keep = (at >= offset) & (at < offset + width)
        br = placed_rows(pad_ref, j, 0, first, offset)
        bi = placed_rows(pad_ref, j, 1, first, offset)
        ar, ai = a_ref_at(0, first), a_ref_at(1, first)
        real = real + jnp.where(keep, ar * br + ai * bi, 0.0)
        imag = imag + jnp.where(keep, ar * bi - ai * br, 0.0)
    return real, imag


def rows_of(parts):
    return jnp.concatenate([jnp.sum(x, axis=0, keepdims=True) for x in parts], axis=0)


def inner_kernel(ro, rw, do, dw, p_ref, x_ref, pad_ref):
    step = pl.program_id(0)
    rows, cols = x_ref.shape[1] // 8, p_ref.shape[1]
    i = rows - 1 - step
    zero = jnp.zeros((8, SIDE), jnp.float32)
    at = pl.ds(pl.multiple_of(i * 8, 8), 8)
    east = [[], []]
    for j in range(cols - 1):
        o, w = ro[i, j], rw[i, j]
        sums = east_sums(
            lambda k: p_ref[0, j, 0, k : k + 32, :],
            lambda k: p_ref[0, j, 1, k : k + 32, :],
            lambda k: pltpu.roll(p_ref[0, j + 1, 0, k : k + 32, :], o, 1),
            lambda k: pltpu.roll(p_ref[0, j + 1, 1, k : k + 32, :], o, 1),
            o,
            w,
        )
        for part in range(2):
            east[part].append(sums[part])
    for part in range(2):
        x_ref[part, at, :] = rows_of(east[part] + [zero])

    @pl.when(step > 0)
    def _():
        south = [[], []]
        for j in range(cols):
            sums = south_sums(
                lambda part, k: p_ref[0, j, part, k : k + 8, :], pad_ref, j, do[i, j], dw[i, j]
            )
            for part in range(2):
                south[part].append(sums[part])
        for part in range(2):
            x_ref[2 + part, at, :] = rows_of(south[part])

    @pl.when(step == 0)
    def _():
        for part in range(2):
            x_ref[2 + part, at, :] = zero

    pad_ref[:, :, PAD : PAD + HALF, :] = p_ref[0, :, :, 0:HALF, :]


def rim_kernel(ro, rw, do, dw, x_ref, col_ref, row_ref, east_ref, south_ref, wide_ref, out_ref, all_ref, pad_ref):
    rows, cols = col_ref.shape[0], row_ref.shape[1]
    pad_ref[:, :, PAD : PAD + HALF, :] = south_ref[...]
    all_ref[...] = x_ref[...]
    for i in range(rows):
        o, w = ro[i, cols - 1], rw[i, cols - 1]
        o2 = jnp.where(o >= HALF, o - HALF, o + HALF)
        sums = east_sums(
            lambda k: col_ref[i, 0, 0, k : k + 32, :],
            lambda k: col_ref[i, 0, 1, k : k + 32, :],
            lambda k: pltpu.roll(east_ref[i, k : k + 32, :], o, 1),
            lambda k: pltpu.roll(east_ref[i, k : k + 32, :], o2, 1),
            o,
            w,
        )
        at = i * cols + cols - 1
        for part in range(2):
            all_ref[part, at : at + 1, :] = jnp.sum(sums[part], axis=0, keepdims=True)
    south = [[], []]
    for j in range(cols):
        sums = south_sums(
            lambda part, k: row_ref[0, j, part, k : k + 8, :],
            pad_ref,
            j,
            do[rows - 1, j],
            dw[rows - 1, j],
        )
        for part in range(2):
            south[part].append(sums[part])
    for part in range(2):
        all_ref[2 + part, (rows - 1) * 8 : rows * 8, :] = rows_of(south[part])
    ones = jnp.ones((8, SIDE), jnp.float32)
    flat = all_ref[...].reshape(4 * rows * cols, SIDE)
    sums = lax.dot_general(
        ones, flat, (((1,), (1,)), ((), ())), precision=HIGHEST, preferred_element_type=jnp.float32
    )
    both = jnp.concatenate([sums[0:1, 0:SIDE], sums[0:1, SIDE : 2 * SIDE]], axis=0)
    out_ref[...] = both / jnp.sqrt(SIDE * wide_ref[...].astype(jnp.float32))


def sync_phases(east, south, n_cols, count):
    lane = lanes(east.shape)
    low = lane < HALF
    col, row = lane % 8, (lane // 8) % 8

    def lane_roll(x, by):
        return pltpu.roll(x, by % SIDE, 1)

    def dev_roll(x, by):
        return pltpu.roll(x, by % x.shape[0], 0)

    def to_east(x):
        return jnp.where(col < 7, lane_roll(x, -1), lane_roll(dev_roll(x, -1), 7))

    def to_west(x):
        return jnp.where(col > 0, lane_roll(x, 1), lane_roll(dev_roll(x, 1), -7))

    def to_south(x):
        return jnp.where(row < 7, lane_roll(x, -8), lane_roll(dev_roll(x, -n_cols), 56))

    def to_north(x):
        return jnp.where(row > 0, lane_roll(x, 8), lane_roll(dev_roll(x, n_cols), -56))

    def swap(x):
        return lane_roll(x, HALF)

    def split(x):
        other = swap(x)
        imag = jnp.where(low, other, x)
        return jnp.where(low, x, other), jnp.where(low, -imag, imag)

    east_r, east_i = split(east)
    south_r, south_i = split(south)
    phase = None
    for step in range(ITERS):
        if step == 0:
            image = east + south
            image = image + to_west(jnp.where(low, east, -east))
            image = image + to_north(jnp.where(low, south, -south))
        else:
            beside, below, other = to_east(phase), to_south(phase), swap(phase)
            image = east_r * beside + east_i * swap(beside)
            image = image + south_r * below + south_i * swap(below)
            image = image + to_west(east_r * phase - east_i * other)
            image = image + to_north(south_r * phase - south_i * other)
        total = jnp.sum(jnp.sum(image * image, axis=0, keepdims=True), axis=1, keepdims=True)
        phase = image / jnp.sqrt(total / count + EPS_NORM)
    return phase


def blend_kernel(
    n_cols, ro, rw, do, dw, me, g_ref, p_ref, east_ref, south_ref, out_ref, phase_ref, all_ref, near_ref, fac, sem, pad_ref
):
    step = pl.program_id(0)
    rows, cols = pl.num_programs(0), p_ref.shape[1]
    i = rows - 1 - step

    @pl.when(step == 0)
    def _():
        n_dev = all_ref.shape[0]
        all_ref[...] = sync_phases(
            g_ref[pl.ds(0, n_dev, 2), :], g_ref[pl.ds(1, n_dev, 2), :], n_cols, n_dev * HALF
        )
        d = me[0]
        lane = lanes((1, SIDE))
        own = all_ref[pl.ds(d, 1), :]
        right = all_ref[pl.ds(lax.rem(d + 1, n_dev), 1), :]
        lower = all_ref[pl.ds(lax.rem(d + n_cols, n_dev), 1), :]
        near_ref[0:1, :] = own
        near_ref[1:2, :] = jnp.where(lane % 8 < 7, pltpu.roll(own, SIDE - 1, 1), pltpu.roll(right, 7, 1))
        near_ref[2:3, :] = jnp.where(
            (lane // 8) % 8 < 7, pltpu.roll(own, SIDE - 8, 1), pltpu.roll(lower, 56, 1)
        )
        copy = pltpu.make_async_copy(near_ref, fac, sem)
        copy.start()
        for part in range(2):
            for k in range(8):
                at = part * HALF + k * 8
                phase_ref[part, k : k + 1, :] = own[:, at : at + 8]
        pad_ref[:, :, PAD : PAD + HALF, :] = south_ref[...]
        copy.wait()

    lane = lanes((8, SIDE))
    row = lax.broadcasted_iota(jnp.int32, (8, SIDE), 0)
    for j in range(cols):
        o, w = ro[i, j], rw[i, j]
        if j == cols - 1:
            w = jnp.where(me[1] > 0, w, 0)
        keep = (lane >= o) & (lane < o + w)
        down = do[i, j]
        deep = jnp.where((me[2] > 0) | (step > 0), dw[i, j], 0)
        at = i * 8 + j
        inv = jnp.where(keep, 0.5, 1.0)
        inv_south = jnp.where(keep, 1.0 / 3.0, 0.5)
        ratio = jnp.where(keep, 2.0 / 3.0, 0.5)
        gr, gi = fac[0, at] * inv, fac[0, HALF + at] * inv
        er = jnp.where(keep, fac[1, at] * 0.5, 0.0)
        ei = jnp.where(keep, fac[1, HALF + at] * 0.5, 0.0)
        sr, si = fac[2, at] * inv_south, fac[2, HALF + at] * inv_south
        o2 = jnp.where(o >= HALF, o - HALF, o + HALF)
        for first in range(0, SIDE, 8):
            rng = slice(first, first + 8)
            ar, ai = p_ref[0, j, 0, rng, :], p_ref[0, j, 1, rng, :]
            if j < cols - 1:
                br = pltpu.roll(p_ref[0, j + 1, 0, rng, :], o, 1)
                bi = pltpu.roll(p_ref[0, j + 1, 1, rng, :], o, 1)
            else:
                br = pltpu.roll(east_ref[0, rng, :], o, 1)
                bi = pltpu.roll(east_ref[0, rng, :], o2, 1)
            real = (gr * ar - gi * ai) + (er * br - ei * bi)
            imag = (gr * ai + gi * ar) + (er * bi + ei * br)
            if first >= ROW0:
                here = row + first
                inside = (here >= down) & (here < down + deep)
                cr = placed_rows(pad_ref, j, 0, first, down)
                ci = placed_rows(pad_ref, j, 1, first, down)
                real = jnp.where(inside, real * ratio + (sr * cr - si * ci), real)
                imag = jnp.where(inside, imag * ratio + (sr * ci + si * cr), imag)
            out_ref[0, j, 0, rng, :] = real
            out_ref[0, j, 1, rng, :] = imag
    pad_ref[:, :, PAD : PAD + HALF, :] = p_ref[0, :, :, 0:HALF, :]


def local(patches, right_offset, right_width, down_offset, down_width):
    rows, cols = patches.shape[:2]
    n_rows, n_cols = lax.axis_size("row"), lax.axis_size("col")
    n_dev = n_rows * n_cols
    r, c = lax.axis_index("row"), lax.axis_index("col")
    tables = (right_offset, right_width, down_offset, down_width)

    strip = jnp.concatenate([patches[:, 0, 0, :, :HALF], patches[:, 0, 1, :, :HALF]], axis=-1)
    east_edge = lax.ppermute(strip, "col", [(k + 1, k) for k in range(n_cols - 1)])
    south_edge = lax.ppermute(patches[0, :, :, :HALF, :], "row", [(k + 1, k) for k in range(n_rows - 1)])

    plane = (2, SIDE, SIDE)
    pad = pltpu.VMEM((cols, 2, PAD + HALF + 8, SIDE), jnp.float32)
    limit = pltpu.CompilerParams(vmem_limit_bytes=24 * 2**20, dimension_semantics=("arbitrary",))
    sums = pl.pallas_call(
        inner_kernel,
        out_shape=jax.ShapeDtypeStruct((4, rows * cols, SIDE), jnp.float32),
        grid_spec=pltpu.PrefetchScalarGridSpec(
            num_scalar_prefetch=4,
            grid=(rows,),
            in_specs=[pl.BlockSpec((1, cols, *plane), lambda s, *_: (rows - 1 - s, 0, 0, 0, 0))],
            out_specs=pl.BlockSpec((4, rows * cols, SIDE), lambda s, *_: (0, 0, 0)),
            scratch_shapes=[pad],
        ),
        compiler_params=limit,
        cost_estimate=pl.CostEstimate(flops=20_000_000, bytes_accessed=9_000_000, transcendentals=0),
        name="inner",
    )(*tables, patches)

    wide = jnp.stack([right_width.reshape(-1), down_width.reshape(-1)])
    wide = jnp.concatenate([wide, wide], axis=1)
    full = lambda shape: pl.BlockSpec(shape, lambda s, *_: (0,) * len(shape))
    corr = pl.pallas_call(
        rim_kernel,
        out_shape=jax.ShapeDtypeStruct((2, SIDE), jnp.float32),
        grid_spec=pltpu.PrefetchScalarGridSpec(
            num_scalar_prefetch=4,
            grid=(1,),
            in_specs=[
                full((4, rows * cols, SIDE)),
                pl.BlockSpec((rows, 1, *plane), lambda s, *_: (0, cols - 1, 0, 0, 0)),
                pl.BlockSpec((1, cols, *plane), lambda s, *_: (rows - 1, 0, 0, 0, 0)),
                full((rows, SIDE, SIDE)),
                full((cols, 2, HALF, SIDE)),
                full((2, SIDE)),
            ],
            out_specs=full((2, SIDE)),
            scratch_shapes=[pltpu.VMEM((4, rows * cols, SIDE), jnp.float32), pad],
        ),
        compiler_params=limit,
        cost_estimate=pl.CostEstimate(flops=5_000_000, bytes_accessed=3_000_000, transcendentals=0),
        name="rim",
    )(*tables, sums, patches, patches, east_edge, south_edge, wide)

    sent = jnp.broadcast_to(corr[None], (n_dev, 2, SIDE)).reshape(n_dev * 2, SIDE)
    grid = lax.all_to_all(sent, ("row", "col"), 0, 0, tiled=True)

    me = jnp.stack([r * n_cols + c, (c < n_cols - 1).astype(jnp.int32), (r < n_rows - 1).astype(jnp.int32)])
    blended, phases = pl.pallas_call(
        functools.partial(blend_kernel, n_cols),
        out_shape=(
            jax.ShapeDtypeStruct(patches.shape, jnp.float32),
            jax.ShapeDtypeStruct((2, rows, cols), jnp.float32),
        ),
        grid_spec=pltpu.PrefetchScalarGridSpec(
            num_scalar_prefetch=5,
            grid=(rows,),
            in_specs=[
                full((n_dev * 2, SIDE)),
                pl.BlockSpec((1, cols, *plane), lambda s, *_: (rows - 1 - s, 0, 0, 0, 0)),
                pl.BlockSpec((1, SIDE, SIDE), lambda s, *_: (rows - 1 - s, 0, 0)),
                full((cols, 2, HALF, SIDE)),
            ],
            out_specs=[
                pl.BlockSpec((1, cols, *plane), lambda s, *_: (rows - 1 - s, 0, 0, 0, 0)),
                full((2, rows, cols)),
            ],
            scratch_shapes=[
                pltpu.VMEM((n_dev, SIDE), jnp.float32),
                pltpu.VMEM((8, SIDE), jnp.float32),
                pltpu.SMEM((8, SIDE), jnp.float32),
                pltpu.SemaphoreType.DMA,
                pad,
            ],
        ),
        compiler_params=limit,
        cost_estimate=pl.CostEstimate(flops=30_000_000, bytes_accessed=18_000_000, transcendentals=0),
        name="blend",
    )(*tables, me, grid, patches, east_edge, south_edge)
    return blended, phases


def solution(mesh):
    return jax.shard_map(
        local,
        mesh=mesh,
        in_specs=(P("row", "col", None, None, None), *(P("row", "col"),) * 4),
        out_specs=(P("row", "col", None, None, None), P(None, "row", "col")),
        check_vma=False,
    )
```

```python
import functools

import jax
import jax.numpy as jnp
from jax import lax
from jax.experimental import pallas as pl
from jax.experimental.pallas import tpu as pltpu
from jax.sharding import PartitionSpec as P

ITERS = 2
EPS_NORM = 1.0
SIDE = 128
HALF = 64
ROW0 = 56
PAD = 8
N = 8
SUMS = 4 * N * N
HIGHEST = lax.Precision.HIGHEST


def lanes(shape):
    return lax.broadcasted_iota(jnp.int32, shape, len(shape) - 1)


def plane(i, j, part):
    return pl.multiple_of(((i * N + j) * 2 + part) * SIDE, SIDE)


def fold8(x):
    total = x[0:8]
    for k in range(8, x.shape[0], 8):
        total = total + x[k : k + 8]
    return total


def other_half(o):
    return jnp.where(o >= HALF, o - HALF, o + HALF)


def east_sums(load_a, load_b, offset, width):
    real, imag = jnp.zeros((8, SIDE), jnp.float32), jnp.zeros((8, SIDE), jnp.float32)
    for k in range(0, SIDE, 32):
        ar, ai, br, bi = load_a(0, k), load_a(1, k), load_b(0, k), load_b(1, k)
        real = real + fold8(ar * br + ai * bi)
        imag = imag + fold8(ar * bi - ai * br)
    lane = lanes((8, SIDE))
    keep = (lane >= offset) & (lane < offset + width)
    return jnp.where(keep, real, 0.0), jnp.where(keep, imag, 0.0)


def south_sums(load_a, load_b, offset, width):
    row = lax.broadcasted_iota(jnp.int32, (8, SIDE), 0)
    real, imag = jnp.zeros((8, SIDE), jnp.float32), jnp.zeros((8, SIDE), jnp.float32)
    for first in range(ROW0, SIDE, 8):
        at = row + first
        keep = (at >= offset) & (at < offset + width)
        start = jnp.maximum(first - offset, -PAD)
        ar, ai, br, bi = load_a(0, first), load_a(1, first), load_b(0, start), load_b(1, start)
        real = real + jnp.where(keep, ar * br + ai * bi, 0.0)
        imag = imag + jnp.where(keep, ar * bi - ai * br, 0.0)
    return real, imag


def fetch_row(p_hbm, p_ref, sems, i):
    block = 2 * N * SIDE
    at = pl.multiple_of(i * block, block)
    return pltpu.make_async_copy(p_hbm.at[pl.ds(at, block), :], p_ref.at[pl.ds(at, block), :], sems.at[i])


def strip_kernel(p_hbm, east_ref, south_ref, col, sems):
    copies = [pltpu.make_async_copy(p_hbm.at[:, 0], col, sems.at[0])]
    copies[0].start()
    for j in range(N):
        for part in range(2):
            at = PAD + (j * 2 + part) * HALF
            copy = pltpu.make_async_copy(
                p_hbm.at[0, j, part, 0:HALF, :], south_ref.at[at : at + HALF, :], sems.at[1 + j * 2 + part]
            )
            copy.start()
            copies.append(copy)
    edge = jnp.zeros((PAD, SIDE), jnp.float32)
    south_ref[0:PAD, :] = edge
    south_ref[PAD + 2 * N * HALF :, :] = edge
    copies[0].wait()
    low = lanes((SIDE, SIDE)) < HALF
    for i in range(N):
        east_ref[i * SIDE : (i + 1) * SIDE, :] = jnp.where(low, col[i, 0], pltpu.roll(col[i, 1], HALF, 1))
    for copy in copies[1:]:
        copy.wait()


def inner_kernel(ro_hbm, rw_hbm, do_hbm, dw_hbm, p_hbm, x_ref, p_ref, ro, rw, do, dw, sems):
    pairs = ((ro_hbm, ro), (rw_hbm, rw), (do_hbm, do), (dw_hbm, dw))
    tables = [pltpu.make_async_copy(a, b, sems.at[N + k]) for k, (a, b) in enumerate(pairs)]
    for copy in tables:
        copy.start()
    for k in range(N):
        fetch_row(p_hbm, p_ref, sems, N - 1 - k).start()
    for copy in tables:
        copy.wait()

    def put(quantity, i, j, value):
        x_ref[pl.ds(quantity * N * N + i * N + j, 8, SUMS), :] = value

    def row_of_patches(step, carry):
        i = N - 1 - step
        fetch_row(p_hbm, p_ref, sems, i).wait()
        for j in range(N - 1):
            o, w = ro[i, j], rw[i, j]
            sums = east_sums(
                lambda part, k: p_ref[pl.ds(plane(i, j, part) + k, 32), :],
                lambda part, k: pltpu.roll(p_ref[pl.ds(plane(i, j + 1, part) + k, 32), :], o, 1),
                o,
                w,
            )
            put(0, i, j, sums[0])
            put(1, i, j, sums[1])

        @pl.when(step > 0)
        def _():
            for j in range(N):
                sums = south_sums(
                    lambda part, k: p_ref[pl.ds(plane(i, j, part) + k, 8), :],
                    lambda part, k: p_ref[pl.ds(plane(i + 1, j, part) + k, 8), :],
                    do[i, j],
                    dw[i, j],
                )
                put(2, i, j, sums[0])
                put(3, i, j, sums[1])

        return carry

    lax.fori_loop(0, N, row_of_patches, 0)


def rim_kernel(ro, rw, do, dw, x_ref, p_ref, east_ref, south_ref, rw_ref, dw_ref, out_ref, all_ref):
    total = x_ref[0:SUMS, :]
    for k in range(1, 8):
        total = total + x_ref[k * SUMS : (k + 1) * SUMS, :]
    all_ref[...] = total

    def put(quantity, i, j, value):
        at = quantity * N * N + i * N + j
        all_ref[at : at + 1, :] = jnp.sum(value, axis=0, keepdims=True)

    for i in range(N):
        o, w = ro[i, N - 1], rw[i, N - 1]
        turn = (o, other_half(o))
        sums = east_sums(
            lambda part, k: p_ref[pl.ds(plane(i, N - 1, part) + k, 32), :],
            lambda part, k: pltpu.roll(east_ref[i * SIDE + k : i * SIDE + k + 32, :], turn[part], 1),
            o,
            w,
        )
        put(0, i, N - 1, sums[0])
        put(1, i, N - 1, sums[1])
    for j in range(N):
        sums = south_sums(
            lambda part, k: p_ref[pl.ds(plane(N - 1, j, part) + k, 8), :],
            lambda part, k: south_ref[pl.ds(PAD + (j * 2 + part) * HALF + k, 8), :],
            do[N - 1, j],
            dw[N - 1, j],
        )
        put(2, N - 1, j, sums[0])
        put(3, N - 1, j, sums[1])
    ones = jnp.ones((8, SIDE), jnp.float32)
    sums = lax.dot_general(
        ones, all_ref[...], (((1,), (1,)), ((), ())), precision=HIGHEST, preferred_element_type=jnp.float32
    )

    def scaled(x, width_ref):
        width = width_ref[...].astype(jnp.float32)
        factor = 1.0 / jnp.sqrt(SIDE * width)
        return x * jnp.concatenate([factor[k : k + 1, :] for k in range(N)] * 2, axis=1)

    east = scaled(sums[0:1, 0:SIDE], rw_ref)
    south = scaled(sums[0:1, SIDE : 2 * SIDE], dw_ref)
    odd = lax.broadcasted_iota(jnp.int32, out_ref.shape, 0) % 2 == 1
    out_ref[...] = jnp.where(odd, south, east)


def sync_phases(east, south, n_cols, count):
    lane = lanes(east.shape)
    low = lane < HALF
    col, row = lane % 8, (lane // 8) % 8

    def lane_roll(x, by):
        return pltpu.roll(x, by % SIDE, 1)

    def dev_roll(x, by):
        return pltpu.roll(x, by % x.shape[0], 0)

    def to_east(x):
        return jnp.where(col < 7, lane_roll(x, -1), lane_roll(dev_roll(x, -1), 7))

    def to_west(x):
        return jnp.where(col > 0, lane_roll(x, 1), lane_roll(dev_roll(x, 1), -7))

    def to_south(x):
        return jnp.where(row < 7, lane_roll(x, -8), lane_roll(dev_roll(x, -n_cols), 56))

    def to_north(x):
        return jnp.where(row > 0, lane_roll(x, 8), lane_roll(dev_roll(x, n_cols), -56))

    def swap(x):
        return lane_roll(x, HALF)

    def split(x):
        other = swap(x)
        imag = jnp.where(low, other, x)
        return jnp.where(low, x, other), jnp.where(low, -imag, imag)

    east_r, east_i = split(east)
    south_r, south_i = split(south)
    phase = None
    for step in range(ITERS):
        if step == 0:
            image = east + south
            image = image + to_west(jnp.where(low, east, -east))
            image = image + to_north(jnp.where(low, south, -south))
        else:
            beside, below, other = to_east(phase), to_south(phase), swap(phase)
            image = east_r * beside + east_i * swap(beside)
            image = image + south_r * below + south_i * swap(below)
            image = image + to_west(east_r * phase - east_i * other)
            image = image + to_north(south_r * phase - south_i * other)
        total = jnp.sum(jnp.sum(image * image, axis=0, keepdims=True), axis=1, keepdims=True)
        phase = image / jnp.sqrt(total / count + EPS_NORM)
    return phase


def blend_kernel(
    n_cols, ro, rw, do, dw, me, g_ref, p_hbm, east_ref, south_ref, out_hbm, phase_ref,
    p_ref, stage, all_ref, near_ref, fac, sem, out_sem, sems,
):
    for i in range(N):
        fetch_row(p_hbm, p_ref, sems, i).start()
    n_dev = all_ref.shape[0]
    all_ref[...] = sync_phases(
        g_ref[pl.ds(0, n_dev, 2), :], g_ref[pl.ds(1, n_dev, 2), :], n_cols, n_dev * N * N
    )
    d = me[0]
    lane = lanes((1, SIDE))
    own = all_ref[pl.ds(d, 1), :]
    right = all_ref[pl.ds(lax.rem(d + 1, n_dev), 1), :]
    lower = all_ref[pl.ds(lax.rem(d + n_cols, n_dev), 1), :]
    near_ref[0:1, :] = own
    near_ref[1:2, :] = jnp.where(lane % 8 < 7, pltpu.roll(own, SIDE - 1, 1), pltpu.roll(right, 7, 1))
    near_ref[2:3, :] = jnp.where(
        (lane // 8) % 8 < 7, pltpu.roll(own, SIDE - 8, 1), pltpu.roll(lower, 56, 1)
    )
    copy = pltpu.make_async_copy(near_ref, fac, sem)
    copy.start()
    for part in range(2):
        for k in range(N):
            at = part * HALF + k * N
            phase_ref[part, k : k + 1, :] = own[:, at : at + N]
    copy.wait()

    lane = lanes((8, SIDE))
    row = lax.broadcasted_iota(jnp.int32, (8, SIDE), 0)

    def row_of_patches(i, last):
        for j in range(N):
            o, w = ro[i, j], rw[i, j]
            if j == N - 1:
                w = jnp.where(me[1] > 0, w, 0)
            keep = (lane >= o) & (lane < o + w)
            down = do[i, j]
            deep = jnp.where(me[2] > 0, dw[i, j], 0) if last else dw[i, j]
            at = i * N + j
            inv = jnp.where(keep, 0.5, 1.0)
            inv_south = jnp.where(keep, 1.0 / 3.0, 0.5)
            ratio = jnp.where(keep, 2.0 / 3.0, 0.5)
            gr, gi = fac[0, at] * inv, fac[0, HALF + at] * inv
            er = jnp.where(keep, fac[1, at] * 0.5, 0.0)
            ei = jnp.where(keep, fac[1, HALF + at] * 0.5, 0.0)
            sr, si = fac[2, at] * inv_south, fac[2, HALF + at] * inv_south
            turn = (o, other_half(o))
            for first in range(0, SIDE, 8):
                ar, ai = (p_ref[pl.ds(plane(i, j, part) + first, 8), :] for part in range(2))
                if j < N - 1:
                    br, bi = (
                        pltpu.roll(p_ref[pl.ds(plane(i, j + 1, part) + first, 8), :], o, 1) for part in range(2)
                    )
                else:
                    both = east_ref[pl.ds(pl.multiple_of(i * SIDE, SIDE) + first, 8), :]
                    br, bi = (pltpu.roll(both, turn[part], 1) for part in range(2))
                real = (gr * ar - gi * ai) + (er * br - ei * bi)
                imag = (gr * ai + gi * ar) + (er * bi + ei * br)
                if first >= ROW0:
                    here = row + first
                    inside = (here >= down) & (here < down + deep)
                    start = jnp.maximum(first - down, -PAD)
                    if last:
                        cr, ci = (south_ref[pl.ds(PAD + (j * 2 + part) * HALF + start, 8), :] for part in range(2))
                    else:
                        cr, ci = (p_ref[pl.ds(plane(i + 1, j, part) + start, 8), :] for part in range(2))
                    real = jnp.where(inside, real * ratio + (sr * cr - si * ci), real)
                    imag = jnp.where(inside, imag * ratio + (sr * ci + si * cr), imag)
                stage[pl.ds(plane(i, j, 0) + first, 8), :] = real
                stage[pl.ds(plane(i, j, 1) + first, 8), :] = imag
            begin = plane(i, j, 0)
            pltpu.make_async_copy(
                stage.at[pl.ds(begin, 2 * SIDE), :], out_hbm.at[pl.ds(begin, 2 * SIDE), :], out_sem
            ).start()

    fetch_row(p_hbm, p_ref, sems, 0).wait()

    def body(i, carry):
        fetch_row(p_hbm, p_ref, sems, i + 1).wait()
        row_of_patches(i, False)
        return carry

    lax.fori_loop(0, N - 1, body, 0)
    row_of_patches(N - 1, True)
    pltpu.make_async_copy(stage, out_hbm, out_sem).wait()


def local(patches, right_offset, right_width, down_offset, down_width):
    n_rows, n_cols = lax.axis_size("row"), lax.axis_size("col")
    n_dev = n_rows * n_cols
    r, c = lax.axis_index("row"), lax.axis_index("col")
    tables = (right_offset, right_width, down_offset, down_width)
    flat_shape = (N * N * 2 * SIDE, SIDE)
    flat = pltpu.with_memory_space_constraint(patches.reshape(flat_shape), pltpu.HBM)
    south_shape = (2 * PAD + N * 2 * HALF, SIDE)
    vmem, smem = pl.BlockSpec(memory_space=pltpu.VMEM), pl.BlockSpec(memory_space=pltpu.SMEM)
    hbm = pl.BlockSpec(memory_space=pltpu.HBM)
    f32 = lambda *shape: jax.ShapeDtypeStruct(shape, jnp.float32)

    def params(mib):
        return pltpu.CompilerParams(vmem_limit_bytes=mib * 2**20)

    def cost(flops, moved):
        return pl.CostEstimate(flops=flops, bytes_accessed=moved, transcendentals=0)

    strip, lower = pl.pallas_call(
        strip_kernel,
        out_shape=(f32(N * SIDE, SIDE), f32(*south_shape)),
        in_specs=[hbm],
        out_specs=(vmem, vmem),
        scratch_shapes=[pltpu.VMEM((N, 2, SIDE, SIDE), jnp.float32), pltpu.SemaphoreType.DMA((1 + 2 * N,))],
        compiler_params=params(8),
        cost_estimate=cost(400_000, 3_000_000),
        name="strips",
    )(pltpu.with_memory_space_constraint(patches, pltpu.HBM))
    east_edge = lax.ppermute(strip, "col", [(k + 1, k) for k in range(n_cols - 1)])
    south_edge = lax.ppermute(lower, "row", [(k + 1, k) for k in range(n_rows - 1)])

    sums, held = pl.pallas_call(
        inner_kernel,
        out_shape=(f32(8 * SUMS, SIDE), f32(*flat_shape)),
        in_specs=[hbm] * 5,
        out_specs=(vmem, vmem),
        scratch_shapes=[pltpu.SMEM((N, N), jnp.int32)] * 4 + [pltpu.SemaphoreType.DMA((N + 4,))],
        compiler_params=params(16),
        cost_estimate=cost(20_000_000, 9_000_000),
        name="inner",
    )(*tables, flat)

    sent = pl.pallas_call(
        rim_kernel,
        out_shape=f32(2 * n_dev, SIDE),
        in_specs=[smem] * 4 + [vmem] * 6,
        out_specs=vmem,
        scratch_shapes=[pltpu.VMEM((SUMS, SIDE), jnp.float32)],
        compiler_params=params(16),
        cost_estimate=cost(5_000_000, 3_000_000),
        name="rim",
    )(*tables, sums, held, east_edge, south_edge, right_width, down_width)
    grid = lax.all_to_all(sent, ("row", "col"), 0, 0, tiled=True)

    me = jnp.stack([r * n_cols + c, (c < n_cols - 1).astype(jnp.int32), (r < n_rows - 1).astype(jnp.int32)])
    blended, phases = pl.pallas_call(
        functools.partial(blend_kernel, n_cols),
        out_shape=(f32(*flat_shape), f32(2, N, N)),
        in_specs=[smem] * 5 + [vmem, hbm, vmem, vmem],
        out_specs=(hbm, vmem),
        scratch_shapes=[
            pltpu.VMEM(flat_shape, jnp.float32),
            pltpu.VMEM(flat_shape, jnp.float32),
            pltpu.VMEM((n_dev, SIDE), jnp.float32),
            pltpu.VMEM((8, SIDE), jnp.float32),
            pltpu.SMEM((8, SIDE), jnp.float32),
            pltpu.SemaphoreType.DMA,
            pltpu.SemaphoreType.DMA,
            pltpu.SemaphoreType.DMA((N,)),
        ],
        compiler_params=params(32),
        cost_estimate=cost(30_000_000, 10_000_000),
        name="blend",
    )(*tables, me, grid, flat, east_edge, south_edge)
    return blended.reshape(patches.shape), phases


def solution(mesh):
    return jax.shard_map(
        local,
        mesh=mesh,
        in_specs=(P("row", "col", None, None, None), *(P("row", "col"),) * 4),
        out_specs=(P("row", "col", None, None, None), P(None, "row", "col")),
        check_vma=False,
    )
```

```python
import functools

import jax
import jax.numpy as jnp
from jax import lax
from jax.experimental import pallas as pl
from jax.experimental.pallas import tpu as pltpu
from jax.sharding import PartitionSpec as P

ITERS = 2
EPS_NORM = 1.0
SIDE = 128
HALF = 64
ROW0 = 56
PAD = 8
N = 8
SUMS = 4 * N * N
HIGHEST = lax.Precision.HIGHEST


def lanes(shape):
    return lax.broadcasted_iota(jnp.int32, shape, len(shape) - 1)


def plane(i, j, part):
    return pl.multiple_of(((i * N + j) * 2 + part) * SIDE, SIDE)


def fold8(x):
    total = x[0:8]
    for k in range(8, x.shape[0], 8):
        total = total + x[k : k + 8]
    return total


def west_slots(lane):
    return (lane % N == N - 1) & ((lane // N) % N >= N // 2)


def other_half(o):
    return jnp.where(o >= HALF, o - HALF, o + HALF)


def east_sums(load_a, load_b, offset, width):
    real, imag = jnp.zeros((8, SIDE), jnp.float32), jnp.zeros((8, SIDE), jnp.float32)
    for k in range(0, SIDE, 32):
        ar, ai, br, bi = load_a(0, k), load_a(1, k), load_b(0, k), load_b(1, k)
        real = real + fold8(ar * br + ai * bi)
        imag = imag + fold8(ar * bi - ai * br)
    lane = lanes((8, SIDE))
    keep = (lane >= offset) & (lane < offset + width)
    return jnp.where(keep, real, 0.0), jnp.where(keep, imag, 0.0)


def south_sums(load_a, load_b, offset, width):
    row = lax.broadcasted_iota(jnp.int32, (8, SIDE), 0)
    real, imag = jnp.zeros((8, SIDE), jnp.float32), jnp.zeros((8, SIDE), jnp.float32)
    for first in range(ROW0, SIDE, 8):
        at = row + first
        keep = (at >= offset) & (at < offset + width)
        start = jnp.maximum(first - offset, -PAD)
        ar, ai, br, bi = load_a(0, first), load_a(1, first), load_b(0, start), load_b(1, start)
        real = real + jnp.where(keep, ar * br + ai * bi, 0.0)
        imag = imag + jnp.where(keep, ar * bi - ai * br, 0.0)
    return real, imag


def fetch_row(p_hbm, p_ref, sems, i):
    block = 2 * N * SIDE
    at = pl.multiple_of(i * block, block)
    return pltpu.make_async_copy(p_hbm.at[pl.ds(at, block), :], p_ref.at[pl.ds(at, block), :], sems.at[i])


def strip_kernel(ro_hbm, rw_hbm, p_hbm, left_ref, right_ref, late_ref, south_ref, first, last, ro, rw, sems):
    half = N // 2
    copies = [
        pltpu.make_async_copy(ro_hbm, ro, sems.at[0]),
        pltpu.make_async_copy(rw_hbm, rw, sems.at[1]),
        pltpu.make_async_copy(p_hbm.at[0:half, 0], first.at[0:half], sems.at[2]),
        pltpu.make_async_copy(p_hbm.at[half:N, N - 1], last, sems.at[3]),
        pltpu.make_async_copy(p_hbm.at[half:N, 0], first.at[half:N], sems.at[4]),
    ]
    for copy in copies:
        copy.start()
    rows = []
    for j in range(N):
        for part in range(2):
            at = PAD + (j * 2 + part) * HALF
            copy = pltpu.make_async_copy(
                p_hbm.at[0, j, part, 0:HALF, :], south_ref.at[at : at + HALF, :], sems.at[5 + j * 2 + part]
            )
            copy.start()
            rows.append(copy)
    edge = jnp.zeros((PAD, SIDE), jnp.float32)
    south_ref[0:PAD, :] = edge
    south_ref[PAD + 2 * N * HALF :, :] = edge
    lane = lanes((SIDE, SIDE))
    low = lane < HALF

    def pack(i):
        return jnp.where(low, first[i, 0], pltpu.roll(first[i, 1], HALF, 1))

    copies[2].wait()
    for i in range(half):
        left_ref[i * SIDE : (i + 1) * SIDE, :] = pack(i)
    copies[0].wait()
    copies[1].wait()
    copies[3].wait()
    for i in range(half):
        o, w = ro[half + i, N - 1], rw[half + i, N - 1]
        scale = 1.0 / jnp.sqrt(SIDE * jnp.full((1, SIDE), w).astype(jnp.float32))
        real = pltpu.roll(last[i, 0], SIDE - o, 1)
        imag = pltpu.roll(last[i, 1], other_half(SIDE - o), 1)
        both = jnp.where(low, real, imag) * scale
        right_ref[i * SIDE : (i + 1) * SIDE, :] = jnp.where(lane % HALF < w, both, 0.0)
    copies[4].wait()
    for i in range(half):
        late_ref[i * SIDE : (i + 1) * SIDE, :] = pack(half + i)
    for copy in rows:
        copy.wait()


def inner_kernel(ro_hbm, rw_hbm, do_hbm, dw_hbm, p_hbm, x_ref, p_ref, ro, rw, do, dw, sems):
    pairs = ((ro_hbm, ro), (rw_hbm, rw), (do_hbm, do), (dw_hbm, dw))
    tables = [pltpu.make_async_copy(a, b, sems.at[N + k]) for k, (a, b) in enumerate(pairs)]
    for copy in tables:
        copy.start()
    for k in range(N):
        fetch_row(p_hbm, p_ref, sems, N - 1 - k).start()
    for copy in tables:
        copy.wait()

    def put(quantity, i, j, value):
        x_ref[pl.ds(quantity * N * N + i * N + j, 8, SUMS), :] = value

    def row_of_patches(step, carry):
        i = N - 1 - step
        fetch_row(p_hbm, p_ref, sems, i).wait()
        for j in range(N - 1):
            o, w = ro[i, j], rw[i, j]
            sums = east_sums(
                lambda part, k: p_ref[pl.ds(plane(i, j, part) + k, 32), :],
                lambda part, k: pltpu.roll(p_ref[pl.ds(plane(i, j + 1, part) + k, 32), :], o, 1),
                o,
                w,
            )
            put(0, i, j, sums[0])
            put(1, i, j, sums[1])

        @pl.when(step > 0)
        def _():
            for j in range(N):
                sums = south_sums(
                    lambda part, k: p_ref[pl.ds(plane(i, j, part) + k, 8), :],
                    lambda part, k: p_ref[pl.ds(plane(i + 1, j, part) + k, 8), :],
                    do[i, j],
                    dw[i, j],
                )
                put(2, i, j, sums[0])
                put(3, i, j, sums[1])

        return carry

    lax.fori_loop(0, N, row_of_patches, 0)


def rim_kernel(ro, rw, do, dw, x_ref, p_ref, east_ref, west_ref, late_ref, south_ref, rw_ref, dw_ref, out_ref, all_ref):
    total = x_ref[0:SUMS, :]
    for k in range(1, 8):
        total = total + x_ref[k * SUMS : (k + 1) * SUMS, :]
    all_ref[...] = total

    def put(quantity, i, j, value):
        at = quantity * N * N + i * N + j
        all_ref[at : at + 1, :] = jnp.sum(value, axis=0, keepdims=True)

    half = N // 2
    low = lanes((32, SIDE)) < HALF
    for i in range(half):
        o, w = ro[i, N - 1], rw[i, N - 1]
        turn = (o, other_half(o))
        sums = east_sums(
            lambda part, k: p_ref[pl.ds(plane(i, N - 1, part) + k, 32), :],
            lambda part, k: pltpu.roll(east_ref[i * SIDE + k : i * SIDE + k + 32, :], turn[part], 1),
            o,
            w,
        )
        put(0, i, N - 1, sums[0])
        put(1, i, N - 1, sums[1])
    for i in range(half):
        real, imag = jnp.zeros((8, SIDE), jnp.float32), jnp.zeros((8, SIDE), jnp.float32)
        for k in range(i * SIDE, (i + 1) * SIDE, 32):
            a, b = west_ref[k : k + 32, :], late_ref[k : k + 32, :]
            cross = a * pltpu.roll(b, HALF, 1)
            real = real + fold8(a * b)
            imag = imag + fold8(jnp.where(low, cross, -cross))
        put(0, half + i, N - 1, real)
        put(1, half + i, N - 1, imag)
    for j in range(N):
        sums = south_sums(
            lambda part, k: p_ref[pl.ds(plane(N - 1, j, part) + k, 8), :],
            lambda part, k: south_ref[pl.ds(PAD + (j * 2 + part) * HALF + k, 8), :],
            do[N - 1, j],
            dw[N - 1, j],
        )
        put(2, N - 1, j, sums[0])
        put(3, N - 1, j, sums[1])
    ones = jnp.ones((8, SIDE), jnp.float32)
    sums = lax.dot_general(
        ones, all_ref[...], (((1,), (1,)), ((), ())), precision=HIGHEST, preferred_element_type=jnp.float32
    )

    def scale_of(width_ref):
        width = width_ref[...].astype(jnp.float32)
        factor = 1.0 / jnp.sqrt(SIDE * width)
        return jnp.concatenate([factor[k : k + 1, :] for k in range(N)] * 2, axis=1)

    foreign = west_slots(lanes((1, SIDE)))
    east = sums[0:1, 0:SIDE] * jnp.where(foreign, 1.0, scale_of(rw_ref))
    south = sums[0:1, SIDE : 2 * SIDE] * scale_of(dw_ref)
    odd = lax.broadcasted_iota(jnp.int32, out_ref.shape, 0) % 2 == 1
    out_ref[...] = jnp.where(odd, south, east)


def sync_phases(east, south, n_cols, count):
    lane = lanes(east.shape)
    low = lane < HALF
    col, row = lane % 8, (lane // 8) % 8

    def lane_roll(x, by):
        return pltpu.roll(x, by % SIDE, 1)

    def dev_roll(x, by):
        return pltpu.roll(x, by % x.shape[0], 0)

    def to_east(x):
        return jnp.where(col < 7, lane_roll(x, -1), lane_roll(dev_roll(x, -1), 7))

    def to_west(x):
        return jnp.where(col > 0, lane_roll(x, 1), lane_roll(dev_roll(x, 1), -7))

    def to_south(x):
        return jnp.where(row < 7, lane_roll(x, -8), lane_roll(dev_roll(x, -n_cols), 56))

    def to_north(x):
        return jnp.where(row > 0, lane_roll(x, 8), lane_roll(dev_roll(x, n_cols), -56))

    def swap(x):
        return lane_roll(x, HALF)

    def split(x):
        other = swap(x)
        imag = jnp.where(low, other, x)
        return jnp.where(low, x, other), jnp.where(low, -imag, imag)

    east = jnp.where(west_slots(lane), dev_roll(east, -1), east)
    east_r, east_i = split(east)
    south_r, south_i = split(south)
    phase = None
    for step in range(ITERS):
        if step == 0:
            image = east + south
            image = image + to_west(jnp.where(low, east, -east))
            image = image + to_north(jnp.where(low, south, -south))
        else:
            beside, below, other = to_east(phase), to_south(phase), swap(phase)
            image = east_r * beside + east_i * swap(beside)
            image = image + south_r * below + south_i * swap(below)
            image = image + to_west(east_r * phase - east_i * other)
            image = image + to_north(south_r * phase - south_i * other)
        total = jnp.sum(jnp.sum(image * image, axis=0, keepdims=True), axis=1, keepdims=True)
        phase = image / jnp.sqrt(total / count + EPS_NORM)
    return phase


def blend_kernel(
    n_cols, ro, rw, do, dw, me, g_ref, p_hbm, left_ref, late_ref, south_ref, out_hbm, phase_ref,
    p_ref, east_ref, stage, all_ref, near_ref, fac, sem, out_sem, sems,
):
    for i in range(N):
        fetch_row(p_hbm, p_ref, sems, i).start()
    size = left_ref.shape[0]
    joins = [
        pltpu.make_async_copy(ref, east_ref.at[k * size : (k + 1) * size, :], sems.at[N + k])
        for k, ref in enumerate((left_ref, late_ref))
    ]
    for join in joins:
        join.start()
    n_dev = all_ref.shape[0]
    all_ref[...] = sync_phases(
        g_ref[pl.ds(0, n_dev, 2), :], g_ref[pl.ds(1, n_dev, 2), :], n_cols, n_dev * N * N
    )
    d = me[0]
    lane = lanes((1, SIDE))
    own = all_ref[pl.ds(d, 1), :]
    right = all_ref[pl.ds(lax.rem(d + 1, n_dev), 1), :]
    lower = all_ref[pl.ds(lax.rem(d + n_cols, n_dev), 1), :]
    near_ref[0:1, :] = own
    near_ref[1:2, :] = jnp.where(lane % 8 < 7, pltpu.roll(own, SIDE - 1, 1), pltpu.roll(right, 7, 1))
    near_ref[2:3, :] = jnp.where(
        (lane // 8) % 8 < 7, pltpu.roll(own, SIDE - 8, 1), pltpu.roll(lower, 56, 1)
    )
    copy = pltpu.make_async_copy(near_ref, fac, sem)
    copy.start()
    for part in range(2):
        for k in range(N):
            at = part * HALF + k * N
            phase_ref[part, k : k + 1, :] = own[:, at : at + N]
    copy.wait()

    lane = lanes((8, SIDE))
    row = lax.broadcasted_iota(jnp.int32, (8, SIDE), 0)

    def row_of_patches(i, last):
        for j in range(N):
            o, w = ro[i, j], rw[i, j]
            if j == N - 1:
                w = jnp.where(me[1] > 0, w, 0)
            keep = (lane >= o) & (lane < o + w)
            down = do[i, j]
            deep = jnp.where(me[2] > 0, dw[i, j], 0) if last else dw[i, j]
            at = i * N + j
            inv = jnp.where(keep, 0.5, 1.0)
            inv_south = jnp.where(keep, 1.0 / 3.0, 0.5)
            ratio = jnp.where(keep, 2.0 / 3.0, 0.5)
            gr, gi = fac[0, at] * inv, fac[0, HALF + at] * inv
            er = jnp.where(keep, fac[1, at] * 0.5, 0.0)
            ei = jnp.where(keep, fac[1, HALF + at] * 0.5, 0.0)
            sr, si = fac[2, at] * inv_south, fac[2, HALF + at] * inv_south
            turn = (o, other_half(o))
            for first in range(0, SIDE, 8):
                ar, ai = (p_ref[pl.ds(plane(i, j, part) + first, 8), :] for part in range(2))
                if j < N - 1:
                    br, bi = (
                        pltpu.roll(p_ref[pl.ds(plane(i, j + 1, part) + first, 8), :], o, 1) for part in range(2)
                    )
                else:
                    both = east_ref[pl.ds(pl.multiple_of(i * SIDE, SIDE) + first, 8), :]
                    br, bi = (pltpu.roll(both, turn[part], 1) for part in range(2))
                real = (gr * ar - gi * ai) + (er * br - ei * bi)
                imag = (gr * ai + gi * ar) + (er * bi + ei * br)
                if first >= ROW0:
                    here = row + first
                    inside = (here >= down) & (here < down + deep)
                    start = jnp.maximum(first - down, -PAD)
                    if last:
                        cr, ci = (south_ref[pl.ds(PAD + (j * 2 + part) * HALF + start, 8), :] for part in range(2))
                    else:
                        cr, ci = (p_ref[pl.ds(plane(i + 1, j, part) + start, 8), :] for part in range(2))
                    real = jnp.where(inside, real * ratio + (sr * cr - si * ci), real)
                    imag = jnp.where(inside, imag * ratio + (sr * ci + si * cr), imag)
                stage[pl.ds(plane(i, j, 0) + first, 8), :] = real
                stage[pl.ds(plane(i, j, 1) + first, 8), :] = imag
            begin = plane(i, j, 0)
            pltpu.make_async_copy(
                stage.at[pl.ds(begin, 2 * SIDE), :], out_hbm.at[pl.ds(begin, 2 * SIDE), :], out_sem
            ).start()

    fetch_row(p_hbm, p_ref, sems, 0).wait()
    for join in joins:
        join.wait()

    def body(i, carry):
        fetch_row(p_hbm, p_ref, sems, i + 1).wait()
        row_of_patches(i, False)
        return carry

    lax.fori_loop(0, N - 1, body, 0)
    row_of_patches(N - 1, True)
    pltpu.make_async_copy(stage, out_hbm, out_sem).wait()


def local(patches, right_offset, right_width, down_offset, down_width):
    n_rows, n_cols = lax.axis_size("row"), lax.axis_size("col")
    n_dev = n_rows * n_cols
    r, c = lax.axis_index("row"), lax.axis_index("col")
    tables = (right_offset, right_width, down_offset, down_width)
    flat_shape = (N * N * 2 * SIDE, SIDE)
    fixed = lambda x: pltpu.with_memory_space_constraint(x, pltpu.HBM)
    flat = fixed(patches.reshape(flat_shape))
    south_shape = (2 * PAD + N * 2 * HALF, SIDE)
    vmem, smem = pl.BlockSpec(memory_space=pltpu.VMEM), pl.BlockSpec(memory_space=pltpu.SMEM)
    hbm = pl.BlockSpec(memory_space=pltpu.HBM)
    f32 = lambda *shape: jax.ShapeDtypeStruct(shape, jnp.float32)

    def params(mib):
        return pltpu.CompilerParams(vmem_limit_bytes=mib * 2**20)

    def cost(flops, moved):
        return pl.CostEstimate(flops=flops, bytes_accessed=moved, transcendentals=0)

    half = N // 2 * SIDE
    left, right, late, lower = pl.pallas_call(
        strip_kernel,
        out_shape=(f32(half, SIDE), f32(half, SIDE), f32(half, SIDE), f32(*south_shape)),
        in_specs=[hbm] * 3,
        out_specs=(vmem,) * 4,
        scratch_shapes=[
            pltpu.VMEM((N, 2, SIDE, SIDE), jnp.float32),
            pltpu.VMEM((N // 2, 2, SIDE, SIDE), jnp.float32),
            pltpu.SMEM((N, N), jnp.int32),
            pltpu.SMEM((N, N), jnp.int32),
            pltpu.SemaphoreType.DMA((5 + 2 * N,)),
        ],
        compiler_params=params(8),
        cost_estimate=cost(400_000, 3_000_000),
        name="strips",
    )(fixed(right_offset), fixed(right_width), fixed(patches))
    to_left = [(k + 1, k) for k in range(n_cols - 1)]
    east_edge = lax.ppermute(left, "col", to_left)
    west_edge = lax.ppermute(right, "col", [(k, k + 1) for k in range(n_cols - 1)])
    south_edge = lax.ppermute(lower, "row", [(k + 1, k) for k in range(n_rows - 1)])

    sums, held = pl.pallas_call(
        inner_kernel,
        out_shape=(f32(8 * SUMS, SIDE), f32(*flat_shape)),
        in_specs=[hbm] * 5,
        out_specs=(vmem, vmem),
        scratch_shapes=[pltpu.SMEM((N, N), jnp.int32)] * 4 + [pltpu.SemaphoreType.DMA((N + 4,))],
        compiler_params=params(16),
        cost_estimate=cost(20_000_000, 9_000_000),
        name="inner",
    )(*map(fixed, tables), flat)

    late, sums = lax.optimization_barrier((late, sums))
    late_edge = lax.ppermute(late, "col", to_left)

    sent = pl.pallas_call(
        rim_kernel,
        out_shape=f32(2 * n_dev, SIDE),
        in_specs=[smem] * 4 + [vmem] * 8,
        out_specs=vmem,
        scratch_shapes=[pltpu.VMEM((SUMS, SIDE), jnp.float32)],
        compiler_params=params(16),
        cost_estimate=cost(5_000_000, 3_000_000),
        name="rim",
    )(*tables, sums, held, east_edge, west_edge, late, south_edge, right_width, down_width)
    grid = lax.all_to_all(sent, ("row", "col"), 0, 0, tiled=True)

    me = jnp.stack([r * n_cols + c, (c < n_cols - 1).astype(jnp.int32), (r < n_rows - 1).astype(jnp.int32)])
    blended, phases = pl.pallas_call(
        functools.partial(blend_kernel, n_cols),
        out_shape=(f32(*flat_shape), f32(2, N, N)),
        in_specs=[smem] * 5 + [vmem, hbm, vmem, vmem, vmem],
        out_specs=(hbm, vmem),
        scratch_shapes=[
            pltpu.VMEM(flat_shape, jnp.float32),
            pltpu.VMEM((N * SIDE, SIDE), jnp.float32),
            pltpu.VMEM(flat_shape, jnp.float32),
            pltpu.VMEM((n_dev, SIDE), jnp.float32),
            pltpu.VMEM((8, SIDE), jnp.float32),
            pltpu.SMEM((8, SIDE), jnp.float32),
            pltpu.SemaphoreType.DMA,
            pltpu.SemaphoreType.DMA,
            pltpu.SemaphoreType.DMA((N + 2,)),
        ],
        compiler_params=params(32),
        cost_estimate=cost(30_000_000, 10_000_000),
        name="blend",
    )(*tables, me, grid, flat, east_edge, late_edge, south_edge)
    return blended.reshape(patches.shape), phases


def solution(mesh):
    return jax.shard_map(
        local,
        mesh=mesh,
        in_specs=(P("row", "col", None, None, None), *(P("row", "col"),) * 4),
        out_specs=(P("row", "col", None, None, None), P(None, "row", "col")),
        check_vma=False,
    )
```

```python
import functools

import jax
import jax.numpy as jnp
from jax import lax
from jax.experimental import pallas as pl
from jax.experimental.pallas import tpu as pltpu
from jax.sharding import PartitionSpec as P

ITERS = 2
EPS_NORM = 1.0
SIDE = 128
HALF = 64
ROW0 = 56
PAD = 8
KEEP = 2
N = 8
SUMS = 4 * N * N
HIGHEST = lax.Precision.HIGHEST


def lanes(shape):
    return lax.broadcasted_iota(jnp.int32, shape, len(shape) - 1)


def plane(i, j, part):
    return pl.multiple_of(((i * N + j) * 2 + part) * SIDE, SIDE)


def fold8(x):
    total = x[0:8]
    for k in range(8, x.shape[0], 8):
        total = total + x[k : k + 8]
    return total


def west_slots(lane):
    return (lane % N == N - 1) & ((lane // N) % N >= N // 2)


def other_half(o):
    return jnp.where(o >= HALF, o - HALF, o + HALF)


def east_sums(load_a, load_b, offset, width):
    real, imag = jnp.zeros((8, SIDE), jnp.float32), jnp.zeros((8, SIDE), jnp.float32)
    for k in range(0, SIDE, 32):
        ar, ai, br, bi = load_a(0, k), load_a(1, k), load_b(0, k), load_b(1, k)
        real = real + fold8(ar * br + ai * bi)
        imag = imag + fold8(ar * bi - ai * br)
    lane = lanes((8, SIDE))
    keep = (lane >= offset) & (lane < offset + width)
    return jnp.where(keep, real, 0.0), jnp.where(keep, imag, 0.0)


def south_sums(load_a, load_b, offset, width):
    row = lax.broadcasted_iota(jnp.int32, (8, SIDE), 0)
    real, imag = jnp.zeros((8, SIDE), jnp.float32), jnp.zeros((8, SIDE), jnp.float32)
    for first in range(ROW0, SIDE, 8):
        at = row + first
        keep = (at >= offset) & (at < offset + width)
        start = jnp.maximum(first - offset, -PAD)
        ar, ai, br, bi = load_a(0, first), load_a(1, first), load_b(0, start), load_b(1, start)
        real = real + jnp.where(keep, ar * br + ai * bi, 0.0)
        imag = imag + jnp.where(keep, ar * bi - ai * br, 0.0)
    return real, imag


def fetch_row(p_hbm, p_ref, sems, i):
    block = 2 * N * SIDE
    at = pl.multiple_of(i * block, block)
    return pltpu.make_async_copy(p_hbm.at[pl.ds(at, block), :], p_ref.at[pl.ds(at, block), :], sems.at[i])


def strip_kernel(ro_hbm, rw_hbm, p_hbm, left_ref, right_ref, late_ref, south_ref, first, last, ro, rw, sems):
    half = N // 2
    copies = [
        pltpu.make_async_copy(ro_hbm, ro, sems.at[0]),
        pltpu.make_async_copy(rw_hbm, rw, sems.at[1]),
        pltpu.make_async_copy(p_hbm.at[0:half, 0], first.at[0:half], sems.at[2]),
        pltpu.make_async_copy(p_hbm.at[half:N, N - 1], last, sems.at[3]),
        pltpu.make_async_copy(p_hbm.at[half:N, 0], first.at[half:N], sems.at[4]),
    ]
    for copy in copies:
        copy.start()
    rows = []
    for j in range(N):
        for part in range(2):
            at = PAD + (j * 2 + part) * HALF
            copy = pltpu.make_async_copy(
                p_hbm.at[0, j, part, 0:HALF, :], south_ref.at[at : at + HALF, :], sems.at[5 + j * 2 + part]
            )
            copy.start()
            rows.append(copy)
    edge = jnp.zeros((PAD, SIDE), jnp.float32)
    south_ref[0:PAD, :] = edge
    south_ref[PAD + 2 * N * HALF :, :] = edge
    lane = lanes((SIDE, SIDE))
    low = lane < HALF

    def pack(i):
        return jnp.where(low, first[i, 0], pltpu.roll(first[i, 1], HALF, 1))

    copies[2].wait()
    for i in range(half):
        left_ref[i * SIDE : (i + 1) * SIDE, :] = pack(i)
    copies[0].wait()
    copies[1].wait()
    copies[3].wait()
    for i in range(half):
        o, w = ro[half + i, N - 1], rw[half + i, N - 1]
        scale = 1.0 / jnp.sqrt(SIDE * jnp.full((1, SIDE), w).astype(jnp.float32))
        real = pltpu.roll(last[i, 0], SIDE - o, 1)
        imag = pltpu.roll(last[i, 1], other_half(SIDE - o), 1)
        both = jnp.where(low, real, imag) * scale
        right_ref[i * SIDE : (i + 1) * SIDE, :] = jnp.where(lane % HALF < w, both, 0.0)
    copies[4].wait()
    for i in range(half):
        late_ref[i * SIDE : (i + 1) * SIDE, :] = pack(half + i)
    for copy in rows:
        copy.wait()


def fetch_tables(refs, scratch, sems):
    copies = [pltpu.make_async_copy(a, b, sems.at[k]) for k, (a, b) in enumerate(zip(refs, scratch))]
    for copy in copies:
        copy.start()
    return copies


def inner_kernel(ro_hbm, rw_hbm, do_hbm, dw_hbm, p_ref, x_ref, keep_ref, ro, rw, do, dw, sems):
    tables = fetch_tables((ro_hbm, rw_hbm, do_hbm, dw_hbm), (ro, rw, do, dw), sems)
    keep = pltpu.make_async_copy(p_ref.at[0 : keep_ref.shape[0], :], keep_ref, sems.at[4])
    keep.start()
    for copy in tables:
        copy.wait()

    def put(quantity, i, j, value):
        x_ref[pl.ds(quantity * N * N + i * N + j, 8, SUMS), :] = value

    def row_of_patches(i, carry):
        for j in range(N - 1):
            o, w = ro[i, j], rw[i, j]
            sums = east_sums(
                lambda part, k: p_ref[pl.ds(plane(i, j, part) + k, 32), :],
                lambda part, k: pltpu.roll(p_ref[pl.ds(plane(i, j + 1, part) + k, 32), :], o, 1),
                o,
                w,
            )
            put(0, i, j, sums[0])
            put(1, i, j, sums[1])

        @pl.when(i < N - 1)
        def _():
            for j in range(N):
                sums = south_sums(
                    lambda part, k: p_ref[pl.ds(plane(i, j, part) + k, 8), :],
                    lambda part, k: p_ref[pl.ds(plane(i + 1, j, part) + k, 8), :],
                    do[i, j],
                    dw[i, j],
                )
                put(2, i, j, sums[0])
                put(3, i, j, sums[1])

        return carry

    lax.fori_loop(0, N, row_of_patches, 0)
    keep.wait()


def rim_kernel(
    ro_hbm, rw_hbm, do_hbm, dw_hbm, x_ref, p_ref, east_ref, west_ref, late_ref, south_ref, rw_ref, dw_ref, out_ref,
    all_ref, ro, rw, do, dw, sems,
):
    tables = fetch_tables((ro_hbm, rw_hbm, do_hbm, dw_hbm), (ro, rw, do, dw), sems)
    total = x_ref[0:SUMS, :]
    for k in range(1, 8):
        total = total + x_ref[k * SUMS : (k + 1) * SUMS, :]
    all_ref[...] = total

    def put(quantity, i, j, value):
        at = quantity * N * N + i * N + j
        all_ref[at : at + 1, :] = jnp.sum(value, axis=0, keepdims=True)

    half = N // 2
    low = lanes((32, SIDE)) < HALF
    for i in range(half):
        real, imag = jnp.zeros((8, SIDE), jnp.float32), jnp.zeros((8, SIDE), jnp.float32)
        for k in range(i * SIDE, (i + 1) * SIDE, 32):
            a, b = west_ref[k : k + 32, :], late_ref[k : k + 32, :]
            cross = a * pltpu.roll(b, HALF, 1)
            real = real + fold8(a * b)
            imag = imag + fold8(jnp.where(low, cross, -cross))
        put(0, half + i, N - 1, real)
        put(1, half + i, N - 1, imag)
    for copy in tables:
        copy.wait()
    for i in range(half):
        o, w = ro[i, N - 1], rw[i, N - 1]
        turn = (o, other_half(o))
        sums = east_sums(
            lambda part, k: p_ref[pl.ds(plane(i, N - 1, part) + k, 32), :],
            lambda part, k: pltpu.roll(east_ref[i * SIDE + k : i * SIDE + k + 32, :], turn[part], 1),
            o,
            w,
        )
        put(0, i, N - 1, sums[0])
        put(1, i, N - 1, sums[1])
    for j in range(N):
        sums = south_sums(
            lambda part, k: p_ref[pl.ds(plane(N - 1, j, part) + k, 8), :],
            lambda part, k: south_ref[pl.ds(PAD + (j * 2 + part) * HALF + k, 8), :],
            do[N - 1, j],
            dw[N - 1, j],
        )
        put(2, N - 1, j, sums[0])
        put(3, N - 1, j, sums[1])
    ones = jnp.ones((8, SIDE), jnp.float32)
    sums = lax.dot_general(
        ones, all_ref[...], (((1,), (1,)), ((), ())), precision=HIGHEST, preferred_element_type=jnp.float32
    )

    def scale_of(width_ref):
        width = width_ref[...].astype(jnp.float32)
        factor = 1.0 / jnp.sqrt(SIDE * width)
        return jnp.concatenate([factor[k : k + 1, :] for k in range(N)] * 2, axis=1)

    foreign = west_slots(lanes((1, SIDE)))
    east = sums[0:1, 0:SIDE] * jnp.where(foreign, 1.0, scale_of(rw_ref))
    south = sums[0:1, SIDE : 2 * SIDE] * scale_of(dw_ref)
    odd = lax.broadcasted_iota(jnp.int32, out_ref.shape, 0) % 2 == 1
    out_ref[...] = jnp.where(odd, south, east)


def sync_phases(east, south, n_cols, count):
    lane = lanes(east.shape)
    low = lane < HALF
    col, row = lane % 8, (lane // 8) % 8

    def lane_roll(x, by):
        return pltpu.roll(x, by % SIDE, 1)

    def dev_roll(x, by):
        return pltpu.roll(x, by % x.shape[0], 0)

    def to_east(x):
        return jnp.where(col < 7, lane_roll(x, -1), lane_roll(dev_roll(x, -1), 7))

    def to_west(x):
        return jnp.where(col > 0, lane_roll(x, 1), lane_roll(dev_roll(x, 1), -7))

    def to_south(x):
        return jnp.where(row < 7, lane_roll(x, -8), lane_roll(dev_roll(x, -n_cols), 56))

    def to_north(x):
        return jnp.where(row > 0, lane_roll(x, 8), lane_roll(dev_roll(x, n_cols), -56))

    def swap(x):
        return lane_roll(x, HALF)

    def split(x):
        other = swap(x)
        imag = jnp.where(low, other, x)
        return jnp.where(low, x, other), jnp.where(low, -imag, imag)

    east = jnp.where(west_slots(lane), dev_roll(east, -1), east)
    east_r, east_i = split(east)
    south_r, south_i = split(south)
    phase = None
    for step in range(ITERS):
        if step == 0:
            image = east + south
            image = image + to_west(jnp.where(low, east, -east))
            image = image + to_north(jnp.where(low, south, -south))
        else:
            beside, below, other = to_east(phase), to_south(phase), swap(phase)
            image = east_r * beside + east_i * swap(beside)
            image = image + south_r * below + south_i * swap(below)
            image = image + to_west(east_r * phase - east_i * other)
            image = image + to_north(south_r * phase - south_i * other)
        total = jnp.sum(jnp.sum(image * image, axis=0, keepdims=True), axis=1, keepdims=True)
        phase = image / jnp.sqrt(total / count + EPS_NORM)
    return phase


def blend_kernel(
    n_rows, n_cols, ro_hbm, rw_hbm, do_hbm, dw_hbm, g_ref, keep_ref, p_hbm, left_ref, late_ref, south_ref, out_hbm, phase_ref,
    p_ref, east_ref, stage, all_ref, near_ref, fac, ro, rw, do, dw, sem, out_sem, sems,
):
    r, c = lax.axis_index("row"), lax.axis_index("col")
    for i in range(KEEP, N):
        fetch_row(p_hbm, p_ref, sems, i).start()
    tables = fetch_tables((ro_hbm, rw_hbm, do_hbm, dw_hbm), (ro, rw, do, dw), sems.at[pl.ds(N + 2, 4)])
    for i in range(KEEP):
        fetch_row(keep_ref, p_ref, sems, i).start()
    size = left_ref.shape[0]
    joins = [
        pltpu.make_async_copy(ref, east_ref.at[k * size : (k + 1) * size, :], sems.at[N + k])
        for k, ref in enumerate((left_ref, late_ref))
    ]
    for join in joins:
        join.start()
    n_dev = all_ref.shape[0]
    all_ref[...] = sync_phases(
        g_ref[pl.ds(0, n_dev, 2), :], g_ref[pl.ds(1, n_dev, 2), :], n_cols, n_dev * N * N
    )
    d = r * n_cols + c
    lane = lanes((1, SIDE))
    own = all_ref[pl.ds(d, 1), :]
    right = all_ref[pl.ds(lax.rem(d + 1, n_dev), 1), :]
    lower = all_ref[pl.ds(lax.rem(d + n_cols, n_dev), 1), :]
    near_ref[0:1, :] = own
    near_ref[1:2, :] = jnp.where(lane % 8 < 7, pltpu.roll(own, SIDE - 1, 1), pltpu.roll(right, 7, 1))
    near_ref[2:3, :] = jnp.where(
        (lane // 8) % 8 < 7, pltpu.roll(own, SIDE - 8, 1), pltpu.roll(lower, 56, 1)
    )
    copy = pltpu.make_async_copy(near_ref, fac, sem)
    copy.start()
    for part in range(2):
        for k in range(N):
            at = part * HALF + k * N
            phase_ref[part, k : k + 1, :] = own[:, at : at + N]
    copy.wait()

    lane = lanes((8, SIDE))
    row = lax.broadcasted_iota(jnp.int32, (8, SIDE), 0)

    def row_of_patches(i, last):
        for j in range(N):
            o, w = ro[i, j], rw[i, j]
            if j == N - 1:
                w = jnp.where(c < n_cols - 1, w, 0)
            keep = (lane >= o) & (lane < o + w)
            down = do[i, j]
            deep = jnp.where(r < n_rows - 1, dw[i, j], 0) if last else dw[i, j]
            at = i * N + j
            inv = jnp.where(keep, 0.5, 1.0)
            inv_south = jnp.where(keep, 1.0 / 3.0, 0.5)
            ratio = jnp.where(keep, 2.0 / 3.0, 0.5)
            gr, gi = fac[0, at] * inv, fac[0, HALF + at] * inv
            er = jnp.where(keep, fac[1, at] * 0.5, 0.0)
            ei = jnp.where(keep, fac[1, HALF + at] * 0.5, 0.0)
            sr, si = fac[2, at] * inv_south, fac[2, HALF + at] * inv_south
            turn = (o, other_half(o))
            for first in range(0, SIDE, 8):
                ar, ai = (p_ref[pl.ds(plane(i, j, part) + first, 8), :] for part in range(2))
                if j < N - 1:
                    br, bi = (
                        pltpu.roll(p_ref[pl.ds(plane(i, j + 1, part) + first, 8), :], o, 1) for part in range(2)
                    )
                else:
                    both = east_ref[pl.ds(pl.multiple_of(i * SIDE, SIDE) + first, 8), :]
                    br, bi = (pltpu.roll(both, turn[part], 1) for part in range(2))
                real = (gr * ar - gi * ai) + (er * br - ei * bi)
                imag = (gr * ai + gi * ar) + (er * bi + ei * br)
                if first >= ROW0:
                    here = row + first
                    inside = (here >= down) & (here < down + deep)
                    start = jnp.maximum(first - down, -PAD)
                    if last:
                        cr, ci = (south_ref[pl.ds(PAD + (j * 2 + part) * HALF + start, 8), :] for part in range(2))
                    else:
                        cr, ci = (p_ref[pl.ds(plane(i + 1, j, part) + start, 8), :] for part in range(2))
                    real = jnp.where(inside, real * ratio + (sr * cr - si * ci), real)
                    imag = jnp.where(inside, imag * ratio + (sr * ci + si * cr), imag)
                stage[pl.ds(plane(i, j, 0) + first, 8), :] = real
                stage[pl.ds(plane(i, j, 1) + first, 8), :] = imag
            begin = plane(i, j, 0)
            pltpu.make_async_copy(
                stage.at[pl.ds(begin, 2 * SIDE), :], out_hbm.at[pl.ds(begin, 2 * SIDE), :], out_sem
            ).start()

    fetch_row(p_hbm, p_ref, sems, 0).wait()
    for join in joins + tables:
        join.wait()

    def body(i, carry):
        fetch_row(p_hbm, p_ref, sems, i + 1).wait()
        row_of_patches(i, False)
        return carry

    lax.fori_loop(0, N - 1, body, 0)
    row_of_patches(N - 1, True)
    pltpu.make_async_copy(stage, out_hbm, out_sem).wait()


def local(patches, right_offset, right_width, down_offset, down_width):
    n_rows, n_cols = lax.axis_size("row"), lax.axis_size("col")
    n_dev = n_rows * n_cols
    tables = (right_offset, right_width, down_offset, down_width)
    flat_shape = (N * N * 2 * SIDE, SIDE)
    fixed = lambda x: pltpu.with_memory_space_constraint(x, pltpu.HBM)
    flat = patches.reshape(flat_shape)
    pinned = [fixed(x) for x in tables]
    table_scratch = [pltpu.SMEM((N, N), jnp.int32)] * 4
    south_shape = (2 * PAD + N * 2 * HALF, SIDE)
    vmem = pl.BlockSpec(memory_space=pltpu.VMEM)
    hbm = pl.BlockSpec(memory_space=pltpu.HBM)
    f32 = lambda *shape: jax.ShapeDtypeStruct(shape, jnp.float32)

    def params(mib):
        return pltpu.CompilerParams(vmem_limit_bytes=mib * 2**20)

    def cost(flops, moved):
        return pl.CostEstimate(flops=flops, bytes_accessed=moved, transcendentals=0)

    half = N // 2 * SIDE
    left, right, late, lower = pl.pallas_call(
        strip_kernel,
        out_shape=(f32(half, SIDE), f32(half, SIDE), f32(half, SIDE), f32(*south_shape)),
        in_specs=[hbm] * 3,
        out_specs=(vmem,) * 4,
        scratch_shapes=[
            pltpu.VMEM((N, 2, SIDE, SIDE), jnp.float32),
            pltpu.VMEM((N // 2, 2, SIDE, SIDE), jnp.float32),
            pltpu.SMEM((N, N), jnp.int32),
            pltpu.SMEM((N, N), jnp.int32),
            pltpu.SemaphoreType.DMA((5 + 2 * N,)),
        ],
        compiler_params=params(8),
        cost_estimate=cost(400_000, 3_000_000),
        name="strips",
    )(fixed(right_offset), fixed(right_width), fixed(patches))
    to_left = [(k + 1, k) for k in range(n_cols - 1)]
    east_edge = lax.ppermute(left, "col", to_left)
    west_edge = lax.ppermute(right, "col", [(k, k + 1) for k in range(n_cols - 1)])
    late_edge = lax.ppermute(late, "col", to_left)
    south_edge = lax.ppermute(lower, "row", [(k + 1, k) for k in range(n_rows - 1)])

    sums, keep = pl.pallas_call(
        inner_kernel,
        out_shape=(f32(8 * SUMS, SIDE), f32(KEEP * N * 2 * SIDE, SIDE)),
        in_specs=[hbm] * 4 + [vmem],
        out_specs=(vmem, vmem),
        scratch_shapes=table_scratch + [pltpu.SemaphoreType.DMA((5,))],
        compiler_params=params(16),
        cost_estimate=cost(20_000_000, 9_000_000),
        name="inner",
    )(*pinned, flat)

    sent = pl.pallas_call(
        rim_kernel,
        out_shape=f32(2 * n_dev, SIDE),
        in_specs=[hbm] * 4 + [vmem] * 8,
        out_specs=vmem,
        scratch_shapes=[pltpu.VMEM((SUMS, SIDE), jnp.float32)] + table_scratch + [pltpu.SemaphoreType.DMA((4,))],
        compiler_params=params(16),
        cost_estimate=cost(5_000_000, 3_000_000),
        name="rim",
    )(*pinned, sums, flat, east_edge, west_edge, late, south_edge, right_width, down_width)
    grid = lax.all_to_all(sent, ("row", "col"), 0, 0, tiled=True)

    blended, phases = pl.pallas_call(
        functools.partial(blend_kernel, n_rows, n_cols),
        out_shape=(f32(*flat_shape), f32(2, N, N)),
        in_specs=[hbm] * 4 + [vmem, vmem, hbm, vmem, vmem, vmem],
        out_specs=(hbm, vmem),
        scratch_shapes=[
            pltpu.VMEM(flat_shape, jnp.float32),
            pltpu.VMEM((N * SIDE, SIDE), jnp.float32),
            pltpu.VMEM(flat_shape, jnp.float32),
            pltpu.VMEM((n_dev, SIDE), jnp.float32),
            pltpu.VMEM((8, SIDE), jnp.float32),
            pltpu.SMEM((8, SIDE), jnp.float32),
            *table_scratch,
            pltpu.SemaphoreType.DMA,
            pltpu.SemaphoreType.DMA,
            pltpu.SemaphoreType.DMA((N + 6,)),
        ],
        compiler_params=params(32),
        cost_estimate=cost(30_000_000, 10_000_000),
        name="blend",
    )(*pinned, grid, keep, fixed(flat), east_edge, late_edge, south_edge)
    return blended.reshape(patches.shape), phases


def solution(mesh):
    return jax.shard_map(
        local,
        mesh=mesh,
        in_specs=(P("row", "col", None, None, None), *(P("row", "col"),) * 4),
        out_specs=(P("row", "col", None, None, None), P(None, "row", "col")),
        check_vma=False,
    )
```

```python
import functools

import jax
import jax.numpy as jnp
from jax import lax
from jax.experimental import pallas as pl
from jax.experimental.pallas import tpu as pltpu
from jax.sharding import PartitionSpec as P

ITERS = 2
EPS_NORM = 1.0
SIDE = 128
HALF = 64
ROW0 = 56
PAD = 8
KEEP = 2
N = 8
SUMS = 4 * N * N
HIGHEST = lax.Precision.HIGHEST


def lanes(shape):
    return lax.broadcasted_iota(jnp.int32, shape, len(shape) - 1)


def plane(i, j, part):
    return pl.multiple_of(((i * N + j) * 2 + part) * SIDE, SIDE)


def fold8(x):
    total = x[0:8]
    for k in range(8, x.shape[0], 8):
        total = total + x[k : k + 8]
    return total


def west_slots(lane):
    return (lane % N == N - 1) & ((lane // N) % N >= N // 2)


def other_half(o):
    return jnp.where(o >= HALF, o - HALF, o + HALF)


def east_sums(load_a, load_b, offset, width):
    real, imag = jnp.zeros((8, SIDE), jnp.float32), jnp.zeros((8, SIDE), jnp.float32)
    for k in range(0, SIDE, 32):
        ar, ai, br, bi = load_a(0, k), load_a(1, k), load_b(0, k), load_b(1, k)
        real = real + fold8(ar * br + ai * bi)
        imag = imag + fold8(ar * bi - ai * br)
    lane = lanes((8, SIDE))
    keep = (lane >= offset) & (lane < offset + width)
    return jnp.where(keep, real, 0.0), jnp.where(keep, imag, 0.0)


def south_sums(load_a, load_b, offset, width):
    row = lax.broadcasted_iota(jnp.int32, (8, SIDE), 0)
    real, imag = jnp.zeros((8, SIDE), jnp.float32), jnp.zeros((8, SIDE), jnp.float32)
    for first in range(ROW0, SIDE, 8):
        at = row + first
        keep = (at >= offset) & (at < offset + width)
        start = jnp.maximum(first - offset, -PAD)
        ar, ai, br, bi = load_a(0, first), load_a(1, first), load_b(0, start), load_b(1, start)
        real = real + jnp.where(keep, ar * br + ai * bi, 0.0)
        imag = imag + jnp.where(keep, ar * bi - ai * br, 0.0)
    return real, imag


def fetch_row(p_hbm, p_ref, sems, i):
    block = 2 * N * SIDE
    at = pl.multiple_of(i * block, block)
    return pltpu.make_async_copy(p_hbm.at[pl.ds(at, block), :], p_ref.at[pl.ds(at, block), :], sems.at[i])


def strip_kernel(
    ro_hbm, rw_hbm, do_hbm, dw_hbm, p_hbm, left_ref, right_ref, late_ref, south_ref, table_ref, first, last, ro, rw, sems
):
    half = N // 2
    copies = [
        pltpu.make_async_copy(ro_hbm, ro, sems.at[0]),
        pltpu.make_async_copy(rw_hbm, rw, sems.at[1]),
        pltpu.make_async_copy(p_hbm.at[0:half, 0], first.at[0:half], sems.at[2]),
        pltpu.make_async_copy(p_hbm.at[half:N, N - 1], last, sems.at[3]),
        pltpu.make_async_copy(p_hbm.at[half:N, 0], first.at[half:N], sems.at[4]),
    ]
    for copy in copies:
        copy.start()
    rows = [
        pltpu.make_async_copy(ref, table_ref.at[k], sems.at[5 + 2 * N + k])
        for k, ref in enumerate((ro_hbm, rw_hbm, do_hbm, dw_hbm))
    ]
    for copy in rows:
        copy.start()
    for j in range(N):
        for part in range(2):
            at = PAD + (j * 2 + part) * HALF
            copy = pltpu.make_async_copy(
                p_hbm.at[0, j, part, 0:HALF, :], south_ref.at[at : at + HALF, :], sems.at[5 + j * 2 + part]
            )
            copy.start()
            rows.append(copy)
    edge = jnp.zeros((PAD, SIDE), jnp.float32)
    south_ref[0:PAD, :] = edge
    south_ref[PAD + 2 * N * HALF :, :] = edge
    lane = lanes((SIDE, SIDE))
    low = lane < HALF

    def pack(i):
        return jnp.where(low, first[i, 0], pltpu.roll(first[i, 1], HALF, 1))

    copies[2].wait()
    for i in range(half):
        left_ref[i * SIDE : (i + 1) * SIDE, :] = pack(i)
    copies[0].wait()
    copies[1].wait()
    copies[3].wait()
    for i in range(half):
        o, w = ro[half + i, N - 1], rw[half + i, N - 1]
        scale = 1.0 / jnp.sqrt(SIDE * jnp.full((1, SIDE), w).astype(jnp.float32))
        real = pltpu.roll(last[i, 0], SIDE - o, 1)
        imag = pltpu.roll(last[i, 1], other_half(SIDE - o), 1)
        both = jnp.where(low, real, imag) * scale
        right_ref[i * SIDE : (i + 1) * SIDE, :] = jnp.where(lane % HALF < w, both, 0.0)
    copies[4].wait()
    for i in range(half):
        late_ref[i * SIDE : (i + 1) * SIDE, :] = pack(half + i)
    for copy in rows:
        copy.wait()


def inner_kernel(table_ref, p_ref, x_ref, keep_ref, table, sems):
    tables = pltpu.make_async_copy(table_ref, table, sems.at[0])
    tables.start()
    keep = pltpu.make_async_copy(p_ref.at[0 : keep_ref.shape[0], :], keep_ref, sems.at[1])
    keep.start()
    tables.wait()
    ro, rw, do, dw = (table.at[k] for k in range(4))

    def put(quantity, i, j, value):
        x_ref[pl.ds(quantity * N * N + i * N + j, 8, SUMS), :] = value

    def row_of_patches(i, carry):
        for j in range(N - 1):
            o, w = ro[i, j], rw[i, j]
            sums = east_sums(
                lambda part, k: p_ref[pl.ds(plane(i, j, part) + k, 32), :],
                lambda part, k: pltpu.roll(p_ref[pl.ds(plane(i, j + 1, part) + k, 32), :], o, 1),
                o,
                w,
            )
            put(0, i, j, sums[0])
            put(1, i, j, sums[1])

        @pl.when(i < N - 1)
        def _():
            for j in range(N):
                sums = south_sums(
                    lambda part, k: p_ref[pl.ds(plane(i, j, part) + k, 8), :],
                    lambda part, k: p_ref[pl.ds(plane(i + 1, j, part) + k, 8), :],
                    do[i, j],
                    dw[i, j],
                )
                put(2, i, j, sums[0])
                put(3, i, j, sums[1])

        return carry

    lax.fori_loop(0, N, row_of_patches, 0)
    keep.wait()


def rim_kernel(
    n_rows, n_cols, table_ref, x_ref, p_ref, east_ref, west_ref, late_ref, south_ref, out_ref, all_ref, table, sem
):
    tables = pltpu.make_async_copy(table_ref, table, sem)
    tables.start()
    ro, rw, do, dw = (table.at[k] for k in range(4))
    r, c = lax.axis_index("row"), lax.axis_index("col")
    total = x_ref[0:SUMS, :]
    for k in range(1, 8):
        total = total + x_ref[k * SUMS : (k + 1) * SUMS, :]
    all_ref[...] = total

    def put(quantity, i, j, value):
        at = quantity * N * N + i * N + j
        all_ref[at : at + 1, :] = jnp.sum(value, axis=0, keepdims=True)

    half = N // 2
    low = lanes((32, SIDE)) < HALF
    for i in range(half):
        real, imag = jnp.zeros((8, SIDE), jnp.float32), jnp.zeros((8, SIDE), jnp.float32)
        for k in range(i * SIDE, (i + 1) * SIDE, 32):
            a, b = west_ref[k : k + 32, :], late_ref[k : k + 32, :]
            cross = a * pltpu.roll(b, HALF, 1)
            real = real + fold8(a * b)
            imag = imag + fold8(jnp.where(low, cross, -cross))
        put(0, half + i, N - 1, jnp.where(c > 0, real, 0.0))
        put(1, half + i, N - 1, jnp.where(c > 0, imag, 0.0))
    tables.wait()
    for i in range(half):
        o, w = ro[i, N - 1], jnp.where(c < n_cols - 1, rw[i, N - 1], 0)
        turn = (o, other_half(o))
        sums = east_sums(
            lambda part, k: p_ref[pl.ds(plane(i, N - 1, part) + k, 32), :],
            lambda part, k: pltpu.roll(east_ref[i * SIDE + k : i * SIDE + k + 32, :], turn[part], 1),
            o,
            w,
        )
        put(0, i, N - 1, sums[0])
        put(1, i, N - 1, sums[1])
    for j in range(N):
        sums = south_sums(
            lambda part, k: p_ref[pl.ds(plane(N - 1, j, part) + k, 8), :],
            lambda part, k: south_ref[pl.ds(PAD + (j * 2 + part) * HALF + k, 8), :],
            do[N - 1, j],
            jnp.where(r < n_rows - 1, dw[N - 1, j], 0),
        )
        put(2, N - 1, j, sums[0])
        put(3, N - 1, j, sums[1])
    ones = jnp.ones((8, SIDE), jnp.float32)
    sums = lax.dot_general(
        ones, all_ref[...], (((1,), (1,)), ((), ())), precision=HIGHEST, preferred_element_type=jnp.float32
    )

    def scale_of(k):
        width = table_ref[k].astype(jnp.float32)
        factor = 1.0 / jnp.sqrt(SIDE * width)
        return jnp.concatenate([factor[k : k + 1, :] for k in range(N)] * 2, axis=1)

    foreign = west_slots(lanes((1, SIDE)))
    east = sums[0:1, 0:SIDE] * jnp.where(foreign, 1.0, scale_of(1))
    south = sums[0:1, SIDE : 2 * SIDE] * scale_of(3)
    odd = lax.broadcasted_iota(jnp.int32, out_ref.shape, 0) % 2 == 1
    out_ref[...] = jnp.where(odd, south, east)


def sync_phases(east, south, n_cols, count):
    lane = lanes(east.shape)
    low = lane < HALF
    col, row = lane % 8, (lane // 8) % 8

    def lane_roll(x, by):
        return pltpu.roll(x, by % SIDE, 1)

    def dev_roll(x, by):
        return pltpu.roll(x, by % x.shape[0], 0)

    def to_east(x):
        return jnp.where(col < 7, lane_roll(x, -1), lane_roll(dev_roll(x, -1), 7))

    def to_west(x):
        return jnp.where(col > 0, lane_roll(x, 1), lane_roll(dev_roll(x, 1), -7))

    def to_south(x):
        return jnp.where(row < 7, lane_roll(x, -8), lane_roll(dev_roll(x, -n_cols), 56))

    def to_north(x):
        return jnp.where(row > 0, lane_roll(x, 8), lane_roll(dev_roll(x, n_cols), -56))

    def swap(x):
        return lane_roll(x, HALF)

    def split(x):
        other = swap(x)
        imag = jnp.where(low, other, x)
        return jnp.where(low, x, other), jnp.where(low, -imag, imag)

    east = jnp.where(west_slots(lane), dev_roll(east, -1), east)
    east_r, east_i = split(east)
    south_r, south_i = split(south)
    phase = None
    for step in range(ITERS):
        if step == 0:
            image = east + south
            image = image + to_west(jnp.where(low, east, -east))
            image = image + to_north(jnp.where(low, south, -south))
        else:
            beside, below, other = to_east(phase), to_south(phase), swap(phase)
            image = east_r * beside + east_i * swap(beside)
            image = image + south_r * below + south_i * swap(below)
            image = image + to_west(east_r * phase - east_i * other)
            image = image + to_north(south_r * phase - south_i * other)
        total = jnp.sum(jnp.sum(image * image, axis=0, keepdims=True), axis=1, keepdims=True)
        phase = image / jnp.sqrt(total / count + EPS_NORM)
    return phase


def blend_kernel(
    n_rows, n_cols, table_ref, g_ref, keep_ref, p_hbm, left_ref, late_ref, south_ref, out_hbm, phase_ref,
    p_ref, east_ref, stage, all_ref, near_ref, fac, table, sem, out_sem, sems,
):
    r, c = lax.axis_index("row"), lax.axis_index("col")
    for i in range(KEEP, N):
        fetch_row(p_hbm, p_ref, sems, i).start()
    tables = pltpu.make_async_copy(table_ref, table, sems.at[N + 2])
    tables.start()
    ro, rw, do, dw = (table.at[k] for k in range(4))
    for i in range(KEEP):
        fetch_row(keep_ref, p_ref, sems, i).start()
    size = left_ref.shape[0]
    joins = [
        pltpu.make_async_copy(ref, east_ref.at[k * size : (k + 1) * size, :], sems.at[N + k])
        for k, ref in enumerate((left_ref, late_ref))
    ]
    for join in joins:
        join.start()
    n_dev = all_ref.shape[0]
    all_ref[...] = sync_phases(
        g_ref[pl.ds(0, n_dev, 2), :], g_ref[pl.ds(1, n_dev, 2), :], n_cols, n_dev * N * N
    )
    d = r * n_cols + c
    lane = lanes((1, SIDE))
    own = all_ref[pl.ds(d, 1), :]
    right = all_ref[pl.ds(lax.rem(d + 1, n_dev), 1), :]
    lower = all_ref[pl.ds(lax.rem(d + n_cols, n_dev), 1), :]
    near_ref[0:1, :] = own
    near_ref[1:2, :] = jnp.where(lane % 8 < 7, pltpu.roll(own, SIDE - 1, 1), pltpu.roll(right, 7, 1))
    near_ref[2:3, :] = jnp.where(
        (lane // 8) % 8 < 7, pltpu.roll(own, SIDE - 8, 1), pltpu.roll(lower, 56, 1)
    )
    copy = pltpu.make_async_copy(near_ref, fac, sem)
    copy.start()
    for part in range(2):
        for k in range(N):
            at = part * HALF + k * N
            phase_ref[part, k : k + 1, :] = own[:, at : at + N]
    copy.wait()

    lane = lanes((8, SIDE))
    row = lax.broadcasted_iota(jnp.int32, (8, SIDE), 0)

    def row_of_patches(i, last):
        for j in range(N):
            o, w = ro[i, j], rw[i, j]
            if j == N - 1:
                w = jnp.where(c < n_cols - 1, w, 0)
            keep = (lane >= o) & (lane < o + w)
            down = do[i, j]
            deep = jnp.where(r < n_rows - 1, dw[i, j], 0) if last else dw[i, j]
            at = i * N + j
            inv = jnp.where(keep, 0.5, 1.0)
            inv_south = jnp.where(keep, 1.0 / 3.0, 0.5)
            ratio = jnp.where(keep, 2.0 / 3.0, 0.5)
            gr, gi = fac[0, at] * inv, fac[0, HALF + at] * inv
            er = jnp.where(keep, fac[1, at] * 0.5, 0.0)
            ei = jnp.where(keep, fac[1, HALF + at] * 0.5, 0.0)
            sr, si = fac[2, at] * inv_south, fac[2, HALF + at] * inv_south
            turn = (o, other_half(o))
            for first in range(0, SIDE, 8):
                ar, ai = (p_ref[pl.ds(plane(i, j, part) + first, 8), :] for part in range(2))
                if j < N - 1:
                    br, bi = (
                        pltpu.roll(p_ref[pl.ds(plane(i, j + 1, part) + first, 8), :], o, 1) for part in range(2)
                    )
                else:
                    both = east_ref[pl.ds(pl.multiple_of(i * SIDE, SIDE) + first, 8), :]
                    br, bi = (pltpu.roll(both, turn[part], 1) for part in range(2))
                real = (gr * ar - gi * ai) + (er * br - ei * bi)
                imag = (gr * ai + gi * ar) + (er * bi + ei * br)
                if first >= ROW0:
                    here = row + first
                    inside = (here >= down) & (here < down + deep)
                    start = jnp.maximum(first - down, -PAD)
                    if last:
                        cr, ci = (south_ref[pl.ds(PAD + (j * 2 + part) * HALF + start, 8), :] for part in range(2))
                    else:
                        cr, ci = (p_ref[pl.ds(plane(i + 1, j, part) + start, 8), :] for part in range(2))
                    real = jnp.where(inside, real * ratio + (sr * cr - si * ci), real)
                    imag = jnp.where(inside, imag * ratio + (sr * ci + si * cr), imag)
                stage[pl.ds(plane(i, j, 0) + first, 8), :] = real
                stage[pl.ds(plane(i, j, 1) + first, 8), :] = imag
            begin = plane(i, j, 0)
            pltpu.make_async_copy(
                stage.at[pl.ds(begin, 2 * SIDE), :], out_hbm.at[pl.ds(begin, 2 * SIDE), :], out_sem
            ).start()

    fetch_row(p_hbm, p_ref, sems, 0).wait()
    for join in joins + [tables]:
        join.wait()

    def body(i, carry):
        fetch_row(p_hbm, p_ref, sems, i + 1).wait()
        row_of_patches(i, False)
        return carry

    lax.fori_loop(0, N - 1, body, 0)
    row_of_patches(N - 1, True)
    pltpu.make_async_copy(stage, out_hbm, out_sem).wait()


def local(patches, right_offset, right_width, down_offset, down_width):
    n_rows, n_cols = lax.axis_size("row"), lax.axis_size("col")
    n_dev = n_rows * n_cols
    tables = (right_offset, right_width, down_offset, down_width)
    flat_shape = (N * N * 2 * SIDE, SIDE)
    fixed = lambda x: pltpu.with_memory_space_constraint(x, pltpu.HBM)
    flat = patches.reshape(flat_shape)
    table_scratch = pltpu.SMEM((4, N, N), jnp.int32)
    south_shape = (2 * PAD + N * 2 * HALF, SIDE)
    vmem = pl.BlockSpec(memory_space=pltpu.VMEM)
    hbm = pl.BlockSpec(memory_space=pltpu.HBM)
    f32 = lambda *shape: jax.ShapeDtypeStruct(shape, jnp.float32)

    def params(mib):
        return pltpu.CompilerParams(vmem_limit_bytes=mib * 2**20)

    def cost(flops, moved):
        return pl.CostEstimate(flops=flops, bytes_accessed=moved, transcendentals=0)

    half = N // 2 * SIDE
    left, right, late, lower, table = pl.pallas_call(
        strip_kernel,
        out_shape=(
            *(f32(half, SIDE),) * 3,
            f32(*south_shape),
            jax.ShapeDtypeStruct((4, N, N), jnp.int32),
        ),
        in_specs=[hbm] * 5,
        out_specs=(vmem,) * 5,
        scratch_shapes=[
            pltpu.VMEM((N, 2, SIDE, SIDE), jnp.float32),
            pltpu.VMEM((N // 2, 2, SIDE, SIDE), jnp.float32),
            pltpu.SMEM((N, N), jnp.int32),
            pltpu.SMEM((N, N), jnp.int32),
            pltpu.SemaphoreType.DMA((9 + 2 * N,)),
        ],
        compiler_params=params(8),
        cost_estimate=cost(400_000, 3_000_000),
        name="strips",
    )(*map(fixed, tables), fixed(patches))
    to_left = [(k, (k - 1) % n_cols) for k in range(n_cols)]
    east_edge = lax.ppermute(left, "col", to_left)
    west_edge = lax.ppermute(right, "col", [(k, (k + 1) % n_cols) for k in range(n_cols)])
    late_edge = lax.ppermute(late, "col", to_left)
    south_edge = lax.ppermute(lower, "row", [(k, (k - 1) % n_rows) for k in range(n_rows)])

    sums, keep = pl.pallas_call(
        inner_kernel,
        out_shape=(f32(8 * SUMS, SIDE), f32(KEEP * N * 2 * SIDE, SIDE)),
        in_specs=[vmem] * 2,
        out_specs=(vmem, vmem),
        scratch_shapes=[table_scratch, pltpu.SemaphoreType.DMA((2,))],
        compiler_params=params(16),
        cost_estimate=cost(20_000_000, 9_000_000),
        name="inner",
    )(table, flat)

    sent = pl.pallas_call(
        functools.partial(rim_kernel, n_rows, n_cols),
        out_shape=f32(2 * n_dev, SIDE),
        in_specs=[vmem] * 7,
        out_specs=vmem,
        scratch_shapes=[pltpu.VMEM((SUMS, SIDE), jnp.float32), table_scratch, pltpu.SemaphoreType.DMA],
        compiler_params=params(16),
        cost_estimate=cost(5_000_000, 3_000_000),
        name="rim",
    )(table, sums, flat, east_edge, west_edge, late, south_edge)
    grid = lax.all_to_all(sent, ("row", "col"), 0, 0, tiled=True)

    blended, phases = pl.pallas_call(
        functools.partial(blend_kernel, n_rows, n_cols),
        out_shape=(f32(*flat_shape), f32(2, N, N)),
        in_specs=[hbm, vmem, vmem, hbm, vmem, vmem, vmem],
        out_specs=(hbm, vmem),
        scratch_shapes=[
            pltpu.VMEM(flat_shape, jnp.float32),
            pltpu.VMEM((N * SIDE, SIDE), jnp.float32),
            pltpu.VMEM(flat_shape, jnp.float32),
            pltpu.VMEM((n_dev, SIDE), jnp.float32),
            pltpu.VMEM((8, SIDE), jnp.float32),
            pltpu.SMEM((8, SIDE), jnp.float32),
            table_scratch,
            pltpu.SemaphoreType.DMA,
            pltpu.SemaphoreType.DMA,
            pltpu.SemaphoreType.DMA((N + 3,)),
        ],
        compiler_params=params(32),
        cost_estimate=cost(30_000_000, 10_000_000),
        name="blend",
    )(fixed(table), grid, keep, fixed(flat), east_edge, late_edge, south_edge)
    return blended.reshape(patches.shape), phases


def solution(mesh):
    return jax.shard_map(
        local,
        mesh=mesh,
        in_specs=(P("row", "col", None, None, None), *(P("row", "col"),) * 4),
        out_specs=(P("row", "col", None, None, None), P(None, "row", "col")),
        check_vma=False,
    )
```

```python
import functools

import jax
import jax.numpy as jnp
from jax import lax
from jax.experimental import pallas as pl
from jax.experimental.pallas import tpu as pltpu
from jax.sharding import PartitionSpec as P

ITERS = 2
EPS_NORM = 1.0
SIDE = 128
HALF = 64
ROW0 = 56
PAD = 8
KEEP = 2
SPLIT = 3
N = 8
SUMS = 4 * N * N
HIGHEST = lax.Precision.HIGHEST


def lanes(shape):
    return lax.broadcasted_iota(jnp.int32, shape, len(shape) - 1)


def plane(i, j, part):
    return pl.multiple_of(((i * N + j) * 2 + part) * SIDE, SIDE)


def fold8(x):
    total = x[0:8]
    for k in range(8, x.shape[0], 8):
        total = total + x[k : k + 8]
    return total


def west_slots(lane):
    return (lane % N == N - 1) & ((lane // N) % N >= SPLIT)


def other_half(o):
    return jnp.where(o >= HALF, o - HALF, o + HALF)


def east_sums(load_a, load_b, offset, width):
    real, imag = jnp.zeros((8, SIDE), jnp.float32), jnp.zeros((8, SIDE), jnp.float32)
    for k in range(0, SIDE, 32):
        ar, ai, br, bi = load_a(0, k), load_a(1, k), load_b(0, k), load_b(1, k)
        real = real + fold8(ar * br + ai * bi)
        imag = imag + fold8(ar * bi - ai * br)
    lane = lanes((8, SIDE))
    keep = (lane >= offset) & (lane < offset + width)
    return jnp.where(keep, real, 0.0), jnp.where(keep, imag, 0.0)


def south_sums(load_a, load_b, offset, width):
    row = lax.broadcasted_iota(jnp.int32, (8, SIDE), 0)
    real, imag = jnp.zeros((8, SIDE), jnp.float32), jnp.zeros((8, SIDE), jnp.float32)
    for first in range(ROW0, SIDE, 8):
        at = row + first
        keep = (at >= offset) & (at < offset + width)
        start = jnp.maximum(first - offset, -PAD)
        ar, ai, br, bi = load_a(0, first), load_a(1, first), load_b(0, start), load_b(1, start)
        real = real + jnp.where(keep, ar * br + ai * bi, 0.0)
        imag = imag + jnp.where(keep, ar * bi - ai * br, 0.0)
    return real, imag


def fetch_row(p_hbm, p_ref, sems, i):
    block = 2 * N * SIDE
    at = pl.multiple_of(i * block, block)
    return pltpu.make_async_copy(p_hbm.at[pl.ds(at, block), :], p_ref.at[pl.ds(at, block), :], sems.at[i])


def strip_kernel(
    ro_hbm, rw_hbm, do_hbm, dw_hbm, p_hbm, left_ref, right_ref, late_ref, south_ref, table_ref, first, last, ro, rw, sems
):
    copies = [
        pltpu.make_async_copy(ro_hbm, ro, sems.at[0]),
        pltpu.make_async_copy(rw_hbm, rw, sems.at[1]),
        pltpu.make_async_copy(p_hbm.at[0:SPLIT, 0], first.at[0:SPLIT], sems.at[2]),
        pltpu.make_async_copy(p_hbm.at[SPLIT:N, N - 1], last, sems.at[3]),
        pltpu.make_async_copy(p_hbm.at[SPLIT:N, 0], first.at[SPLIT:N], sems.at[4]),
    ]
    for copy in copies:
        copy.start()
    rows = [
        pltpu.make_async_copy(ref, table_ref.at[k], sems.at[5 + 2 * N + k])
        for k, ref in enumerate((ro_hbm, rw_hbm, do_hbm, dw_hbm))
    ]
    for copy in rows:
        copy.start()
    for j in range(N):
        for part in range(2):
            at = PAD + (j * 2 + part) * HALF
            copy = pltpu.make_async_copy(
                p_hbm.at[0, j, part, 0:HALF, :], south_ref.at[at : at + HALF, :], sems.at[5 + j * 2 + part]
            )
            copy.start()
            rows.append(copy)
    edge = jnp.zeros((PAD, SIDE), jnp.float32)
    south_ref[0:PAD, :] = edge
    south_ref[PAD + 2 * N * HALF :, :] = edge
    lane = lanes((SIDE, SIDE))
    low = lane < HALF

    def pack(i):
        return jnp.where(low, first[i, 0], pltpu.roll(first[i, 1], HALF, 1))

    copies[2].wait()
    for i in range(SPLIT):
        left_ref[i * SIDE : (i + 1) * SIDE, :] = pack(i)
    copies[0].wait()
    copies[1].wait()
    copies[3].wait()
    for i in range(N - SPLIT):
        o, w = ro[SPLIT + i, N - 1], rw[SPLIT + i, N - 1]
        scale = 1.0 / jnp.sqrt(SIDE * jnp.full((1, SIDE), w).astype(jnp.float32))
        real = pltpu.roll(last[i, 0], SIDE - o, 1)
        imag = pltpu.roll(last[i, 1], other_half(SIDE - o), 1)
        both = jnp.where(low, real, imag) * scale
        right_ref[i * SIDE : (i + 1) * SIDE, :] = jnp.where(lane % HALF < w, both, 0.0)
    copies[4].wait()
    for i in range(N - SPLIT):
        late_ref[i * SIDE : (i + 1) * SIDE, :] = pack(SPLIT + i)
    for copy in rows:
        copy.wait()


def inner_kernel(table_ref, p_ref, x_ref, keep_ref, table, sems):
    tables = pltpu.make_async_copy(table_ref, table, sems.at[0])
    tables.start()
    keep = pltpu.make_async_copy(p_ref.at[0 : keep_ref.shape[0], :], keep_ref, sems.at[1])
    keep.start()
    tables.wait()
    ro, rw, do, dw = (table.at[k] for k in range(4))

    def put(quantity, i, j, value):
        x_ref[pl.ds(quantity * N * N + i * N + j, 8, SUMS), :] = value

    def row_of_patches(i, carry):
        for j in range(N - 1):
            o, w = ro[i, j], rw[i, j]
            sums = east_sums(
                lambda part, k: p_ref[pl.ds(plane(i, j, part) + k, 32), :],
                lambda part, k: pltpu.roll(p_ref[pl.ds(plane(i, j + 1, part) + k, 32), :], o, 1),
                o,
                w,
            )
            put(0, i, j, sums[0])
            put(1, i, j, sums[1])

        @pl.when(i < N - 1)
        def _():
            for j in range(N):
                sums = south_sums(
                    lambda part, k: p_ref[pl.ds(plane(i, j, part) + k, 8), :],
                    lambda part, k: p_ref[pl.ds(plane(i + 1, j, part) + k, 8), :],
                    do[i, j],
                    dw[i, j],
                )
                put(2, i, j, sums[0])
                put(3, i, j, sums[1])

        return carry

    lax.fori_loop(0, N, row_of_patches, 0)
    keep.wait()


def rim_kernel(
    n_rows, n_cols, table_ref, x_ref, p_ref, east_ref, west_ref, late_ref, south_ref, out_ref, all_ref, table, sem
):
    tables = pltpu.make_async_copy(table_ref, table, sem)
    tables.start()
    ro, rw, do, dw = (table.at[k] for k in range(4))
    r, c = lax.axis_index("row"), lax.axis_index("col")
    total = x_ref[0:SUMS, :]
    for k in range(1, 8):
        total = total + x_ref[k * SUMS : (k + 1) * SUMS, :]
    all_ref[...] = total

    def put(quantity, i, j, value):
        at = quantity * N * N + i * N + j
        all_ref[at : at + 1, :] = jnp.sum(value, axis=0, keepdims=True)

    low = lanes((32, SIDE)) < HALF
    for i in range(N - SPLIT):
        real, imag = jnp.zeros((8, SIDE), jnp.float32), jnp.zeros((8, SIDE), jnp.float32)
        for k in range(i * SIDE, (i + 1) * SIDE, 32):
            a, b = west_ref[k : k + 32, :], late_ref[k : k + 32, :]
            cross = a * pltpu.roll(b, HALF, 1)
            real = real + fold8(a * b)
            imag = imag + fold8(jnp.where(low, cross, -cross))
        put(0, SPLIT + i, N - 1, jnp.where(c > 0, real, 0.0))
        put(1, SPLIT + i, N - 1, jnp.where(c > 0, imag, 0.0))
    tables.wait()
    for i in range(SPLIT):
        o, w = ro[i, N - 1], jnp.where(c < n_cols - 1, rw[i, N - 1], 0)
        turn = (o, other_half(o))
        sums = east_sums(
            lambda part, k: p_ref[pl.ds(plane(i, N - 1, part) + k, 32), :],
            lambda part, k: pltpu.roll(east_ref[i * SIDE + k : i * SIDE + k + 32, :], turn[part], 1),
            o,
            w,
        )
        put(0, i, N - 1, sums[0])
        put(1, i, N - 1, sums[1])
    for j in range(N):
        sums = south_sums(
            lambda part, k: p_ref[pl.ds(plane(N - 1, j, part) + k, 8), :],
            lambda part, k: south_ref[pl.ds(PAD + (j * 2 + part) * HALF + k, 8), :],
            do[N - 1, j],
            jnp.where(r < n_rows - 1, dw[N - 1, j], 0),
        )
        put(2, N - 1, j, sums[0])
        put(3, N - 1, j, sums[1])
    ones = jnp.ones((8, SIDE), jnp.float32)
    sums = lax.dot_general(
        ones, all_ref[...], (((1,), (1,)), ((), ())), precision=HIGHEST, preferred_element_type=jnp.float32
    )

    def scale_of(k):
        width = table_ref[k].astype(jnp.float32)
        factor = 1.0 / jnp.sqrt(SIDE * width)
        return jnp.concatenate([factor[k : k + 1, :] for k in range(N)] * 2, axis=1)

    foreign = west_slots(lanes((1, SIDE)))
    east = sums[0:1, 0:SIDE] * jnp.where(foreign, 1.0, scale_of(1))
    south = sums[0:1, SIDE : 2 * SIDE] * scale_of(3)
    odd = lax.broadcasted_iota(jnp.int32, out_ref.shape, 0) % 2 == 1
    out_ref[...] = jnp.where(odd, south, east)


def sync_phases(east, south, n_cols, count):
    lane = lanes(east.shape)
    low = lane < HALF
    col, row = lane % 8, (lane // 8) % 8

    def lane_roll(x, by):
        return pltpu.roll(x, by % SIDE, 1)

    def dev_roll(x, by):
        return pltpu.roll(x, by % x.shape[0], 0)

    def to_east(x):
        return jnp.where(col < 7, lane_roll(x, -1), lane_roll(dev_roll(x, -1), 7))

    def to_west(x):
        return jnp.where(col > 0, lane_roll(x, 1), lane_roll(dev_roll(x, 1), -7))

    def to_south(x):
        return jnp.where(row < 7, lane_roll(x, -8), lane_roll(dev_roll(x, -n_cols), 56))

    def to_north(x):
        return jnp.where(row > 0, lane_roll(x, 8), lane_roll(dev_roll(x, n_cols), -56))

    def swap(x):
        return lane_roll(x, HALF)

    def split(x):
        other = swap(x)
        imag = jnp.where(low, other, x)
        return jnp.where(low, x, other), jnp.where(low, -imag, imag)

    east = jnp.where(west_slots(lane), dev_roll(east, -1), east)
    east_r, east_i = split(east)
    south_r, south_i = split(south)
    phase = None
    for step in range(ITERS):
        if step == 0:
            image = east + south
            image = image + to_west(jnp.where(low, east, -east))
            image = image + to_north(jnp.where(low, south, -south))
        else:
            beside, below, other = to_east(phase), to_south(phase), swap(phase)
            image = east_r * beside + east_i * swap(beside)
            image = image + south_r * below + south_i * swap(below)
            image = image + to_west(east_r * phase - east_i * other)
            image = image + to_north(south_r * phase - south_i * other)
        total = jnp.sum(jnp.sum(image * image, axis=0, keepdims=True), axis=1, keepdims=True)
        phase = image / jnp.sqrt(total / count + EPS_NORM)
    return phase


def blend_kernel(
    n_rows, n_cols, table_ref, g_ref, keep_ref, p_hbm, left_ref, late_ref, south_ref, out_hbm, phase_ref,
    p_ref, east_ref, stage, all_ref, near_ref, fac, table, sem, out_sem, sems,
):
    r, c = lax.axis_index("row"), lax.axis_index("col")
    for i in range(KEEP, N):
        fetch_row(p_hbm, p_ref, sems, i).start()
    tables = pltpu.make_async_copy(table_ref, table, sems.at[N + 2])
    tables.start()
    ro, rw, do, dw = (table.at[k] for k in range(4))
    for i in range(KEEP):
        fetch_row(keep_ref, p_ref, sems, i).start()
    size = left_ref.shape[0]
    joins = [
        pltpu.make_async_copy(left_ref, east_ref.at[0:size, :], sems.at[N]),
        pltpu.make_async_copy(late_ref, east_ref.at[size : N * SIDE, :], sems.at[N + 1]),
    ]
    for join in joins:
        join.start()
    n_dev = all_ref.shape[0]
    all_ref[...] = sync_phases(
        g_ref[pl.ds(0, n_dev, 2), :], g_ref[pl.ds(1, n_dev, 2), :], n_cols, n_dev * N * N
    )
    d = r * n_cols + c
    lane = lanes((1, SIDE))
    own = all_ref[pl.ds(d, 1), :]
    right = all_ref[pl.ds(lax.rem(d + 1, n_dev), 1), :]
    lower = all_ref[pl.ds(lax.rem(d + n_cols, n_dev), 1), :]
    near_ref[0:1, :] = own
    near_ref[1:2, :] = jnp.where(lane % 8 < 7, pltpu.roll(own, SIDE - 1, 1), pltpu.roll(right, 7, 1))
    near_ref[2:3, :] = jnp.where(
        (lane // 8) % 8 < 7, pltpu.roll(own, SIDE - 8, 1), pltpu.roll(lower, 56, 1)
    )
    copy = pltpu.make_async_copy(near_ref, fac, sem)
    copy.start()
    for part in range(2):
        for k in range(N):
            at = part * HALF + k * N
            phase_ref[part, k : k + 1, :] = own[:, at : at + N]
    copy.wait()

    lane = lanes((8, SIDE))
    row = lax.broadcasted_iota(jnp.int32, (8, SIDE), 0)

    def row_of_patches(i, last):
        for j in range(N):
            o, w = ro[i, j], rw[i, j]
            if j == N - 1:
                w = jnp.where(c < n_cols - 1, w, 0)
            keep = (lane >= o) & (lane < o + w)
            down = do[i, j]
            deep = jnp.where(r < n_rows - 1, dw[i, j], 0) if last else dw[i, j]
            at = i * N + j
            inv = jnp.where(keep, 0.5, 1.0)
            inv_south = jnp.where(keep, 1.0 / 3.0, 0.5)
            ratio = jnp.where(keep, 2.0 / 3.0, 0.5)
            gr, gi = fac[0, at] * inv, fac[0, HALF + at] * inv
            er = jnp.where(keep, fac[1, at] * 0.5, 0.0)
            ei = jnp.where(keep, fac[1, HALF + at] * 0.5, 0.0)
            sr, si = fac[2, at] * inv_south, fac[2, HALF + at] * inv_south
            turn = (o, other_half(o))
            for first in range(0, SIDE, 8):
                ar, ai = (p_ref[pl.ds(plane(i, j, part) + first, 8), :] for part in range(2))
                if j < N - 1:
                    br, bi = (
                        pltpu.roll(p_ref[pl.ds(plane(i, j + 1, part) + first, 8), :], o, 1) for part in range(2)
                    )
                else:
                    both = east_ref[pl.ds(pl.multiple_of(i * SIDE, SIDE) + first, 8), :]
                    br, bi = (pltpu.roll(both, turn[part], 1) for part in range(2))
                real = (gr * ar - gi * ai) + (er * br - ei * bi)
                imag = (gr * ai + gi * ar) + (er * bi + ei * br)
                if first >= ROW0:
                    here = row + first
                    inside = (here >= down) & (here < down + deep)
                    start = jnp.maximum(first - down, -PAD)
                    if last:
                        cr, ci = (south_ref[pl.ds(PAD + (j * 2 + part) * HALF + start, 8), :] for part in range(2))
                    else:
                        cr, ci = (p_ref[pl.ds(plane(i + 1, j, part) + start, 8), :] for part in range(2))
                    real = jnp.where(inside, real * ratio + (sr * cr - si * ci), real)
                    imag = jnp.where(inside, imag * ratio + (sr * ci + si * cr), imag)
                stage[pl.ds(plane(i, j, 0) + first, 8), :] = real
                stage[pl.ds(plane(i, j, 1) + first, 8), :] = imag
            begin = plane(i, j, 0)
            pltpu.make_async_copy(
                stage.at[pl.ds(begin, 2 * SIDE), :], out_hbm.at[pl.ds(begin, 2 * SIDE), :], out_sem
            ).start()

    fetch_row(p_hbm, p_ref, sems, 0).wait()
    for join in joins + [tables]:
        join.wait()

    def body(i, carry):
        fetch_row(p_hbm, p_ref, sems, i + 1).wait()
        row_of_patches(i, False)
        return carry

    lax.fori_loop(0, N - 1, body, 0)
    row_of_patches(N - 1, True)
    pltpu.make_async_copy(stage, out_hbm, out_sem).wait()


def local(patches, right_offset, right_width, down_offset, down_width):
    n_rows, n_cols = lax.axis_size("row"), lax.axis_size("col")
    n_dev = n_rows * n_cols
    tables = (right_offset, right_width, down_offset, down_width)
    flat_shape = (N * N * 2 * SIDE, SIDE)
    fixed = lambda x: pltpu.with_memory_space_constraint(x, pltpu.HBM)
    flat = patches.reshape(flat_shape)
    table_scratch = pltpu.SMEM((4, N, N), jnp.int32)
    south_shape = (2 * PAD + N * 2 * HALF, SIDE)
    vmem = pl.BlockSpec(memory_space=pltpu.VMEM)
    hbm = pl.BlockSpec(memory_space=pltpu.HBM)
    f32 = lambda *shape: jax.ShapeDtypeStruct(shape, jnp.float32)

    def params(mib):
        return pltpu.CompilerParams(vmem_limit_bytes=mib * 2**20)

    def cost(flops, moved):
        return pl.CostEstimate(flops=flops, bytes_accessed=moved, transcendentals=0)

    near, far = SPLIT * SIDE, (N - SPLIT) * SIDE
    left, right, late, lower, table = pl.pallas_call(
        strip_kernel,
        out_shape=(
            f32(near, SIDE),
            f32(far, SIDE),
            f32(far, SIDE),
            f32(*south_shape),
            jax.ShapeDtypeStruct((4, N, N), jnp.int32),
        ),
        in_specs=[hbm] * 5,
        out_specs=(vmem,) * 5,
        scratch_shapes=[
            pltpu.VMEM((N, 2, SIDE, SIDE), jnp.float32),
            pltpu.VMEM((N - SPLIT, 2, SIDE, SIDE), jnp.float32),
            pltpu.SMEM((N, N), jnp.int32),
            pltpu.SMEM((N, N), jnp.int32),
            pltpu.SemaphoreType.DMA((9 + 2 * N,)),
        ],
        compiler_params=params(8),
        cost_estimate=cost(400_000, 3_000_000),
        name="strips",
    )(*map(fixed, tables), fixed(patches))
    to_left = [(k, (k - 1) % n_cols) for k in range(n_cols)]
    east_edge = lax.ppermute(left, "col", to_left)
    west_edge = lax.ppermute(right, "col", [(k, (k + 1) % n_cols) for k in range(n_cols)])
    south_edge = lax.ppermute(lower, "row", [(k, (k - 1) % n_rows) for k in range(n_rows)])

    sums, keep = pl.pallas_call(
        inner_kernel,
        out_shape=(f32(8 * SUMS, SIDE), f32(KEEP * N * 2 * SIDE, SIDE)),
        in_specs=[vmem] * 2,
        out_specs=(vmem, vmem),
        scratch_shapes=[table_scratch, pltpu.SemaphoreType.DMA((2,))],
        compiler_params=params(16),
        cost_estimate=cost(20_000_000, 9_000_000),
        name="inner",
    )(table, flat)

    sent = pl.pallas_call(
        functools.partial(rim_kernel, n_rows, n_cols),
        out_shape=f32(2 * n_dev, SIDE),
        in_specs=[vmem] * 7,
        out_specs=vmem,
        scratch_shapes=[pltpu.VMEM((SUMS, SIDE), jnp.float32), table_scratch, pltpu.SemaphoreType.DMA],
        compiler_params=params(16),
        cost_estimate=cost(5_000_000, 3_000_000),
        name="rim",
    )(table, sums, flat, east_edge, west_edge, late, south_edge)
    late_out, sent = lax.optimization_barrier((late, sent))
    late_edge = lax.ppermute(late_out, "col", to_left)
    grid = lax.all_to_all(sent, ("row", "col"), 0, 0, tiled=True)

    blended, phases = pl.pallas_call(
        functools.partial(blend_kernel, n_rows, n_cols),
        out_shape=(f32(*flat_shape), f32(2, N, N)),
        in_specs=[hbm, vmem, vmem, hbm, vmem, vmem, vmem],
        out_specs=(hbm, vmem),
        scratch_shapes=[
            pltpu.VMEM(flat_shape, jnp.float32),
            pltpu.VMEM((N * SIDE, SIDE), jnp.float32),
            pltpu.VMEM(flat_shape, jnp.float32),
            pltpu.VMEM((n_dev, SIDE), jnp.float32),
            pltpu.VMEM((8, SIDE), jnp.float32),
            pltpu.SMEM((8, SIDE), jnp.float32),
            table_scratch,
            pltpu.SemaphoreType.DMA,
            pltpu.SemaphoreType.DMA,
            pltpu.SemaphoreType.DMA((N + 3,)),
        ],
        compiler_params=params(32),
        cost_estimate=cost(30_000_000, 10_000_000),
        name="blend",
    )(fixed(table), grid, keep, fixed(flat), east_edge, late_edge, south_edge)
    return blended.reshape(patches.shape), phases


def solution(mesh):
    return jax.shard_map(
        local,
        mesh=mesh,
        in_specs=(P("row", "col", None, None, None), *(P("row", "col"),) * 4),
        out_specs=(P("row", "col", None, None, None), P(None, "row", "col")),
        check_vma=False,
    )
```

```python
import functools

import jax
import jax.numpy as jnp
from jax import lax
from jax.experimental import pallas as pl
from jax.experimental.pallas import tpu as pltpu
from jax.sharding import PartitionSpec as P

ITERS = 2
EPS_NORM = 1.0
SIDE = 128
HALF = 64
ROW0 = 56
PAD = 8
KEEP = 2
SPLIT = 3
N = 8
SUMS = 4 * N * N
HIGHEST = lax.Precision.HIGHEST


def lanes(shape):
    return lax.broadcasted_iota(jnp.int32, shape, len(shape) - 1)


def plane(i, j, part):
    return pl.multiple_of(((i * N + j) * 2 + part) * SIDE, SIDE)


def fold8(x):
    total = x[0:8]
    for k in range(8, x.shape[0], 8):
        total = total + x[k : k + 8]
    return total


def west_slots(lane):
    return (lane % N == N - 1) & ((lane // N) % N >= SPLIT)


def other_half(o):
    return jnp.where(o >= HALF, o - HALF, o + HALF)


def east_sums(load_a, load_b, offset, width):
    real, imag = jnp.zeros((8, SIDE), jnp.float32), jnp.zeros((8, SIDE), jnp.float32)
    for k in range(0, SIDE, 32):
        ar, ai, br, bi = load_a(0, k), load_a(1, k), load_b(0, k), load_b(1, k)
        real = real + fold8(ar * br + ai * bi)
        imag = imag + fold8(ar * bi - ai * br)
    lane = lanes((8, SIDE))
    keep = (lane >= offset) & (lane < offset + width)
    return jnp.where(keep, real, 0.0), jnp.where(keep, imag, 0.0)


def south_sums(load_a, load_b, offset, width):
    row = lax.broadcasted_iota(jnp.int32, (8, SIDE), 0)
    real, imag = jnp.zeros((8, SIDE), jnp.float32), jnp.zeros((8, SIDE), jnp.float32)
    for first in range(ROW0, SIDE, 8):
        at = row + first
        keep = (at >= offset) & (at < offset + width)
        start = jnp.maximum(first - offset, -PAD)
        ar, ai, br, bi = load_a(0, first), load_a(1, first), load_b(0, start), load_b(1, start)
        real = real + jnp.where(keep, ar * br + ai * bi, 0.0)
        imag = imag + jnp.where(keep, ar * bi - ai * br, 0.0)
    return real, imag


def fetch_row(p_hbm, p_ref, sems, i):
    block = 2 * N * SIDE
    at = pl.multiple_of(i * block, block)
    return pltpu.make_async_copy(p_hbm.at[pl.ds(at, block), :], p_ref.at[pl.ds(at, block), :], sems.at[i])


def strip_kernel(
    ro_hbm, rw_hbm, do_hbm, dw_hbm, p_hbm, left_ref, right_ref, south_ref, table_ref, first, last, ro, rw, sems
):
    copies = [
        pltpu.make_async_copy(ro_hbm, ro, sems.at[0]),
        pltpu.make_async_copy(rw_hbm, rw, sems.at[1]),
        pltpu.make_async_copy(p_hbm.at[0:SPLIT, 0], first.at[0:SPLIT], sems.at[2]),
        pltpu.make_async_copy(p_hbm.at[SPLIT:N, N - 1], last, sems.at[3]),
    ]
    for copy in copies:
        copy.start()
    rows = [
        pltpu.make_async_copy(ref, table_ref.at[k], sems.at[4 + 2 * N + k])
        for k, ref in enumerate((ro_hbm, rw_hbm, do_hbm, dw_hbm))
    ]
    for copy in rows:
        copy.start()
    for j in range(N):
        for part in range(2):
            at = PAD + (j * 2 + part) * HALF
            copy = pltpu.make_async_copy(
                p_hbm.at[0, j, part, 0:HALF, :], south_ref.at[at : at + HALF, :], sems.at[4 + j * 2 + part]
            )
            copy.start()
            rows.append(copy)
    edge = jnp.zeros((PAD, SIDE), jnp.float32)
    south_ref[0:PAD, :] = edge
    south_ref[PAD + 2 * N * HALF :, :] = edge
    lane = lanes((SIDE, SIDE))
    low = lane < HALF

    def pack(i):
        return jnp.where(low, first[i, 0], pltpu.roll(first[i, 1], HALF, 1))

    copies[2].wait()
    for i in range(SPLIT):
        left_ref[i * SIDE : (i + 1) * SIDE, :] = pack(i)
    copies[0].wait()
    copies[1].wait()
    copies[3].wait()
    for i in range(N - SPLIT):
        o, w = ro[SPLIT + i, N - 1], rw[SPLIT + i, N - 1]
        scale = 1.0 / jnp.sqrt(SIDE * jnp.full((1, SIDE), w).astype(jnp.float32))
        real = pltpu.roll(last[i, 0], SIDE - o, 1)
        imag = pltpu.roll(last[i, 1], other_half(SIDE - o), 1)
        both = jnp.where(low, real, imag) * scale
        right_ref[i * SIDE : (i + 1) * SIDE, :] = jnp.where(lane % HALF < w, both, 0.0)
    for copy in rows:
        copy.wait()


def inner_kernel(table_ref, p_ref, sum_ref, keep_ref, late_ref, x_ref, table, sems):
    tables = pltpu.make_async_copy(table_ref, table, sems.at[0])
    tables.start()
    keep = pltpu.make_async_copy(p_ref.at[0 : keep_ref.shape[0], :], keep_ref, sems.at[1])
    keep.start()
    low = lanes((SIDE, SIDE)) < HALF
    for i in range(SPLIT, N):
        real, imag = (p_ref[pl.ds(plane(i, 0, part), SIDE), :] for part in range(2))
        at = (i - SPLIT) * SIDE
        late_ref[at : at + SIDE, :] = jnp.where(low, real, pltpu.roll(imag, HALF, 1))
    tables.wait()
    ro, rw, do, dw = (table.at[k] for k in range(4))

    def put(quantity, i, j, value):
        x_ref[pl.ds(quantity * N * N + i * N + j, 8, SUMS), :] = value

    def row_of_patches(i, carry):
        for j in range(N - 1):
            o, w = ro[i, j], rw[i, j]
            sums = east_sums(
                lambda part, k: p_ref[pl.ds(plane(i, j, part) + k, 32), :],
                lambda part, k: pltpu.roll(p_ref[pl.ds(plane(i, j + 1, part) + k, 32), :], o, 1),
                o,
                w,
            )
            put(0, i, j, sums[0])
            put(1, i, j, sums[1])

        @pl.when(i < N - 1)
        def _():
            for j in range(N):
                sums = south_sums(
                    lambda part, k: p_ref[pl.ds(plane(i, j, part) + k, 8), :],
                    lambda part, k: p_ref[pl.ds(plane(i + 1, j, part) + k, 8), :],
                    do[i, j],
                    dw[i, j],
                )
                put(2, i, j, sums[0])
                put(3, i, j, sums[1])

        return carry

    lax.fori_loop(0, N, row_of_patches, 0)
    total = x_ref[0:SUMS, :]
    for k in range(1, 8):
        total = total + x_ref[k * SUMS : (k + 1) * SUMS, :]
    sum_ref[...] = total
    keep.wait()


def rim_kernel(
    n_rows, n_cols, table_ref, x_ref, p_ref, east_ref, west_ref, late_ref, south_ref, out_ref, all_ref, table, sem
):
    tables = pltpu.make_async_copy(table_ref, table, sem)
    tables.start()
    ro, rw, do, dw = (table.at[k] for k in range(4))
    r, c = lax.axis_index("row"), lax.axis_index("col")
    all_ref[...] = x_ref[...]

    def put(quantity, i, j, value):
        at = quantity * N * N + i * N + j
        all_ref[at : at + 1, :] = jnp.sum(value, axis=0, keepdims=True)

    low = lanes((32, SIDE)) < HALF
    for i in range(N - SPLIT):
        real, imag = jnp.zeros((8, SIDE), jnp.float32), jnp.zeros((8, SIDE), jnp.float32)
        for k in range(i * SIDE, (i + 1) * SIDE, 32):
            a, b = west_ref[k : k + 32, :], late_ref[k : k + 32, :]
            cross = a * pltpu.roll(b, HALF, 1)
            real = real + fold8(a * b)
            imag = imag + fold8(jnp.where(low, cross, -cross))
        put(0, SPLIT + i, N - 1, jnp.where(c > 0, real, 0.0))
        put(1, SPLIT + i, N - 1, jnp.where(c > 0, imag, 0.0))
    tables.wait()
    for i in range(SPLIT):
        o, w = ro[i, N - 1], jnp.where(c < n_cols - 1, rw[i, N - 1], 0)
        turn = (o, other_half(o))
        sums = east_sums(
            lambda part, k: p_ref[pl.ds(plane(i, N - 1, part) + k, 32), :],
            lambda part, k: pltpu.roll(east_ref[i * SIDE + k : i * SIDE + k + 32, :], turn[part], 1),
            o,
            w,
        )
        put(0, i, N - 1, sums[0])
        put(1, i, N - 1, sums[1])
    for j in range(N):
        sums = south_sums(
            lambda part, k: p_ref[pl.ds(plane(N - 1, j, part) + k, 8), :],
            lambda part, k: south_ref[pl.ds(PAD + (j * 2 + part) * HALF + k, 8), :],
            do[N - 1, j],
            jnp.where(r < n_rows - 1, dw[N - 1, j], 0),
        )
        put(2, N - 1, j, sums[0])
        put(3, N - 1, j, sums[1])
    ones = jnp.ones((8, SIDE), jnp.float32)
    sums = lax.dot_general(
        ones, all_ref[...], (((1,), (1,)), ((), ())), precision=HIGHEST, preferred_element_type=jnp.float32
    )

    def scale_of(k):
        width = table_ref[k].astype(jnp.float32)
        factor = 1.0 / jnp.sqrt(SIDE * width)
        return jnp.concatenate([factor[k : k + 1, :] for k in range(N)] * 2, axis=1)

    foreign = west_slots(lanes((1, SIDE)))
    east = sums[0:1, 0:SIDE] * jnp.where(foreign, 1.0, scale_of(1))
    south = sums[0:1, SIDE : 2 * SIDE] * scale_of(3)
    odd = lax.broadcasted_iota(jnp.int32, out_ref.shape, 0) % 2 == 1
    out_ref[...] = jnp.where(odd, south, east)


def sync_phases(east, south, n_cols, count):
    lane = lanes(east.shape)
    low = lane < HALF
    col, row = lane % 8, (lane // 8) % 8

    def lane_roll(x, by):
        return pltpu.roll(x, by % SIDE, 1)

    def dev_roll(x, by):
        return pltpu.roll(x, by % x.shape[0], 0)

    def to_east(x):
        return jnp.where(col < 7, lane_roll(x, -1), lane_roll(dev_roll(x, -1), 7))

    def to_west(x):
        return jnp.where(col > 0, lane_roll(x, 1), lane_roll(dev_roll(x, 1), -7))

    def to_south(x):
        return jnp.where(row < 7, lane_roll(x, -8), lane_roll(dev_roll(x, -n_cols), 56))

    def to_north(x):
        return jnp.where(row > 0, lane_roll(x, 8), lane_roll(dev_roll(x, n_cols), -56))

    def swap(x):
        return lane_roll(x, HALF)

    def split(x):
        other = swap(x)
        imag = jnp.where(low, other, x)
        return jnp.where(low, x, other), jnp.where(low, -imag, imag)

    east = jnp.where(west_slots(lane), dev_roll(east, -1), east)
    east_r, east_i = split(east)
    south_r, south_i = split(south)
    phase = None
    for step in range(ITERS):
        if step == 0:
            image = east + south
            image = image + to_west(jnp.where(low, east, -east))
            image = image + to_north(jnp.where(low, south, -south))
        else:
            beside, below, other = to_east(phase), to_south(phase), swap(phase)
            image = east_r * beside + east_i * swap(beside)
            image = image + south_r * below + south_i * swap(below)
            image = image + to_west(east_r * phase - east_i * other)
            image = image + to_north(south_r * phase - south_i * other)
        total = jnp.sum(jnp.sum(image * image, axis=0, keepdims=True), axis=1, keepdims=True)
        phase = image / jnp.sqrt(total / count + EPS_NORM)
    return phase


def blend_kernel(
    n_rows, n_cols, table_ref, g_ref, keep_ref, p_hbm, left_ref, late_ref, south_ref, out_hbm, phase_ref,
    p_ref, east_ref, stage, all_ref, near_ref, fac, table, sem, out_sem, sems,
):
    r, c = lax.axis_index("row"), lax.axis_index("col")
    for i in range(KEEP, N):
        fetch_row(p_hbm, p_ref, sems, i).start()
    tables = pltpu.make_async_copy(table_ref, table, sems.at[N + 2])
    tables.start()
    ro, rw, do, dw = (table.at[k] for k in range(4))
    for i in range(KEEP):
        fetch_row(keep_ref, p_ref, sems, i).start()
    size = left_ref.shape[0]
    joins = [
        pltpu.make_async_copy(left_ref, east_ref.at[0:size, :], sems.at[N]),
        pltpu.make_async_copy(late_ref, east_ref.at[size : N * SIDE, :], sems.at[N + 1]),
    ]
    for join in joins:
        join.start()
    n_dev = all_ref.shape[0]
    all_ref[...] = sync_phases(
        g_ref[pl.ds(0, n_dev, 2), :], g_ref[pl.ds(1, n_dev, 2), :], n_cols, n_dev * N * N
    )
    d = r * n_cols + c
    lane = lanes((1, SIDE))
    own = all_ref[pl.ds(d, 1), :]
    right = all_ref[pl.ds(lax.rem(d + 1, n_dev), 1), :]
    lower = all_ref[pl.ds(lax.rem(d + n_cols, n_dev), 1), :]
    near_ref[0:1, :] = own
    near_ref[1:2, :] = jnp.where(lane % 8 < 7, pltpu.roll(own, SIDE - 1, 1), pltpu.roll(right, 7, 1))
    near_ref[2:3, :] = jnp.where(
        (lane // 8) % 8 < 7, pltpu.roll(own, SIDE - 8, 1), pltpu.roll(lower, 56, 1)
    )
    copy = pltpu.make_async_copy(near_ref, fac, sem)
    copy.start()
    for part in range(2):
        for k in range(N):
            at = part * HALF + k * N
            phase_ref[part, k : k + 1, :] = own[:, at : at + N]
    copy.wait()

    lane = lanes((8, SIDE))
    row = lax.broadcasted_iota(jnp.int32, (8, SIDE), 0)

    def row_of_patches(i, last):
        for j in range(N):
            o, w = ro[i, j], rw[i, j]
            if j == N - 1:
                w = jnp.where(c < n_cols - 1, w, 0)
            keep = (lane >= o) & (lane < o + w)
            down = do[i, j]
            deep = jnp.where(r < n_rows - 1, dw[i, j], 0) if last else dw[i, j]
            at = i * N + j
            inv = jnp.where(keep, 0.5, 1.0)
            inv_south = jnp.where(keep, 1.0 / 3.0, 0.5)
            ratio = jnp.where(keep, 2.0 / 3.0, 0.5)
            gr, gi = fac[0, at] * inv, fac[0, HALF + at] * inv
            er = jnp.where(keep, fac[1, at] * 0.5, 0.0)
            ei = jnp.where(keep, fac[1, HALF + at] * 0.5, 0.0)
            sr, si = fac[2, at] * inv_south, fac[2, HALF + at] * inv_south
            turn = (o, other_half(o))
            for first in range(0, SIDE, 8):
                ar, ai = (p_ref[pl.ds(plane(i, j, part) + first, 8), :] for part in range(2))
                if j < N - 1:
                    br, bi = (
                        pltpu.roll(p_ref[pl.ds(plane(i, j + 1, part) + first, 8), :], o, 1) for part in range(2)
                    )
                else:
                    both = east_ref[pl.ds(pl.multiple_of(i * SIDE, SIDE) + first, 8), :]
                    br, bi = (pltpu.roll(both, turn[part], 1) for part in range(2))
                real = (gr * ar - gi * ai) + (er * br - ei * bi)
                imag = (gr * ai + gi * ar) + (er * bi + ei * br)
                if first >= ROW0:
                    here = row + first
                    inside = (here >= down) & (here < down + deep)
                    start = jnp.maximum(first - down, -PAD)
                    if last:
                        cr, ci = (south_ref[pl.ds(PAD + (j * 2 + part) * HALF + start, 8), :] for part in range(2))
                    else:
                        cr, ci = (p_ref[pl.ds(plane(i + 1, j, part) + start, 8), :] for part in range(2))
                    real = jnp.where(inside, real * ratio + (sr * cr - si * ci), real)
                    imag = jnp.where(inside, imag * ratio + (sr * ci + si * cr), imag)
                stage[pl.ds(plane(i, j, 0) + first, 8), :] = real
                stage[pl.ds(plane(i, j, 1) + first, 8), :] = imag
            begin = plane(i, j, 0)
            pltpu.make_async_copy(
                stage.at[pl.ds(begin, 2 * SIDE), :], out_hbm.at[pl.ds(begin, 2 * SIDE), :], out_sem
            ).start()

    fetch_row(p_hbm, p_ref, sems, 0).wait()
    for join in joins + [tables]:
        join.wait()

    def body(i, carry):
        fetch_row(p_hbm, p_ref, sems, i + 1).wait()
        row_of_patches(i, False)
        return carry

    lax.fori_loop(0, N - 1, body, 0)
    row_of_patches(N - 1, True)
    pltpu.make_async_copy(stage, out_hbm, out_sem).wait()


def local(patches, right_offset, right_width, down_offset, down_width):
    n_rows, n_cols = lax.axis_size("row"), lax.axis_size("col")
    n_dev = n_rows * n_cols
    tables = (right_offset, right_width, down_offset, down_width)
    flat_shape = (N * N * 2 * SIDE, SIDE)
    fixed = lambda x: pltpu.with_memory_space_constraint(x, pltpu.HBM)
    flat = patches.reshape(flat_shape)
    table_scratch = pltpu.SMEM((4, N, N), jnp.int32)
    south_shape = (2 * PAD + N * 2 * HALF, SIDE)
    vmem = pl.BlockSpec(memory_space=pltpu.VMEM)
    hbm = pl.BlockSpec(memory_space=pltpu.HBM)
    f32 = lambda *shape: jax.ShapeDtypeStruct(shape, jnp.float32)

    def params(mib):
        return pltpu.CompilerParams(vmem_limit_bytes=mib * 2**20)

    def cost(flops, moved):
        return pl.CostEstimate(flops=flops, bytes_accessed=moved, transcendentals=0)

    near, far = SPLIT * SIDE, (N - SPLIT) * SIDE
    left, right, lower, table = pl.pallas_call(
        strip_kernel,
        out_shape=(
            f32(near, SIDE),
            f32(far, SIDE),
            f32(*south_shape),
            jax.ShapeDtypeStruct((4, N, N), jnp.int32),
        ),
        in_specs=[hbm] * 5,
        out_specs=(vmem,) * 4,
        scratch_shapes=[
            pltpu.VMEM((SPLIT, 2, SIDE, SIDE), jnp.float32),
            pltpu.VMEM((N - SPLIT, 2, SIDE, SIDE), jnp.float32),
            pltpu.SMEM((N, N), jnp.int32),
            pltpu.SMEM((N, N), jnp.int32),
            pltpu.SemaphoreType.DMA((8 + 2 * N,)),
        ],
        compiler_params=params(8),
        cost_estimate=cost(400_000, 3_000_000),
        name="strips",
    )(*map(fixed, tables), fixed(patches))
    to_left = [(k, (k - 1) % n_cols) for k in range(n_cols)]
    east_edge = lax.ppermute(left, "col", to_left)
    west_edge = lax.ppermute(right, "col", [(k, (k + 1) % n_cols) for k in range(n_cols)])
    south_edge = lax.ppermute(lower, "row", [(k, (k - 1) % n_rows) for k in range(n_rows)])

    sums, keep, late = pl.pallas_call(
        inner_kernel,
        out_shape=(f32(SUMS, SIDE), f32(KEEP * N * 2 * SIDE, SIDE), f32(far, SIDE)),
        in_specs=[vmem] * 2,
        out_specs=(vmem,) * 3,
        scratch_shapes=[pltpu.VMEM((8 * SUMS, SIDE), jnp.float32), table_scratch, pltpu.SemaphoreType.DMA((2,))],
        compiler_params=params(16),
        cost_estimate=cost(20_000_000, 9_000_000),
        name="inner",
    )(table, flat)

    sent = pl.pallas_call(
        functools.partial(rim_kernel, n_rows, n_cols),
        out_shape=f32(2 * n_dev, SIDE),
        in_specs=[vmem] * 7,
        out_specs=vmem,
        scratch_shapes=[pltpu.VMEM((SUMS, SIDE), jnp.float32), table_scratch, pltpu.SemaphoreType.DMA],
        compiler_params=params(16),
        cost_estimate=cost(5_000_000, 3_000_000),
        name="rim",
    )(table, sums, flat, east_edge, west_edge, late, south_edge)
    late_out, sent = lax.optimization_barrier((late, sent))
    late_edge = lax.ppermute(late_out, "col", to_left)
    grid = lax.all_to_all(sent, ("row", "col"), 0, 0, tiled=True)

    blended, phases = pl.pallas_call(
        functools.partial(blend_kernel, n_rows, n_cols),
        out_shape=(f32(*flat_shape), f32(2, N, N)),
        in_specs=[hbm, vmem, vmem, hbm, vmem, vmem, vmem],
        out_specs=(hbm, vmem),
        scratch_shapes=[
            pltpu.VMEM(flat_shape, jnp.float32),
            pltpu.VMEM((N * SIDE, SIDE), jnp.float32),
            pltpu.VMEM(flat_shape, jnp.float32),
            pltpu.VMEM((n_dev, SIDE), jnp.float32),
            pltpu.VMEM((8, SIDE), jnp.float32),
            pltpu.SMEM((8, SIDE), jnp.float32),
            table_scratch,
            pltpu.SemaphoreType.DMA,
            pltpu.SemaphoreType.DMA,
            pltpu.SemaphoreType.DMA((N + 3,)),
        ],
        compiler_params=params(32),
        cost_estimate=cost(30_000_000, 10_000_000),
        name="blend",
    )(fixed(table), grid, keep, fixed(flat), east_edge, late_edge, south_edge)
    return blended.reshape(patches.shape), phases


def solution(mesh):
    return jax.shard_map(
        local,
        mesh=mesh,
        in_specs=(P("row", "col", None, None, None), *(P("row", "col"),) * 4),
        out_specs=(P("row", "col", None, None, None), P(None, "row", "col")),
        check_vma=False,
    )
```
